32 devices in a mesh: ctx: 8 (over y, x, core), kv: 4 (over z).
Axes of the slice: x: 2, y: 2, z: 4, core: 2. Of those that a mesh axis runs over, the one named last changes fastest.
Arguments:
- prompt_in: bfloat16 [128, 8192], P(None, 'ctx'), may hold values from -6 to 6
- step_in: bfloat16 [3, 32, 8192], P(None, None, 'ctx'), may hold values from -6 to 6
- norm_gain: bfloat16 [8192], P('ctx'), may hold values from 0.099609375 to 1.8984375
- query_weight: bfloat16 [8192, 4096], P('ctx', 'kv'), may hold values from -0.125 to 0.125
- key_weight: bfloat16 [8192, 512], P('ctx', 'kv'), may hold values from -0.125 to 0.125
- value_weight: bfloat16 [8192, 512], P('ctx', 'kv'), may hold values from -0.0625 to 0.0625
- out_weight: bfloat16 [4096, 8192], P('kv', 'ctx'), may hold values from -0.125 to 0.125
- key_cache: bfloat16 [4, 65536, 128], P('kv', 'ctx'), may hold values from -540 to 540
- value_cache: bfloat16 [4, 65536, 128], P('kv', 'ctx'), may hold values from -5 to 5
- cache_lengths: int32 [8], P('ctx'), may hold values from 2048 to 8192
- visible: int32 [32], replicated, may hold values from 1 to 128, as said below
Outputs:
- prompt_out: bfloat16 [128, 8192], P('kv', 'ctx')
- step_out: bfloat16 [3, 32, 8192], P(None, 'kv', 'ctx')
The draws below stay inside these ranges and needn't reach their ends.
Inputs may be any that keep to these rules, and one draw needn't show every extreme that they name: `visible`: prompt tokens seen by each decode row.
All inputs are finite; a program needn't handle non-finite values.
Results may differ from the reference program's by a relative error of at most 0.035.
Values may be sent and summed in bfloat16 or wider, within the bound.
No kernel may reach another device: no remote copies, remote signals or barrier semaphores. Data moves between devices by JAX's collectives and lax.ppermute only.
A program may use at most 192 MiB of HBM per device.

```python
import jax
import jax.numpy as jnp
from jax import lax

D = 8192
HD = 128
QPK = 8
KV_HEADS = 4
CACHE_DEV = 8192
PROMPT_DEV = 16
ROWS_DEV = 4
STEPS = 3
SHARDS = 8
CACHE = 65536
PROMPT = 128
ROWS = 32


def draw_key_cache(key, part):
    entries = jnp.clip(jax.random.normal(key, (KV_HEADS, CACHE, HD), jnp.float32), -6.0, 6.0) * 1.5
    return entries.astype(jnp.bfloat16)


def draw_value_cache(key, part):
    jitter = jnp.clip(jax.random.normal(key, (KV_HEADS, SHARDS, CACHE_DEV, HD), jnp.float32), -4.0, 4.0)
    centers = jax.random.uniform(jax.random.fold_in(key, 21), (KV_HEADS, SHARDS, 1, HD), jnp.float32, -1.0, 1.0)
    return (jitter + centers).reshape(KV_HEADS, CACHE, HD).astype(jnp.bfloat16)


def draw_cache_lengths(key, part):
    lengths = jax.random.randint(key, (SHARDS,), CACHE_DEV // 4, CACHE_DEV + 1)
    full_shard = jax.random.randint(jax.random.fold_in(key, 31), (), 0, SHARDS)
    short_shard = (full_shard + 1 + jax.random.randint(jax.random.fold_in(key, 32), (), 0, SHARDS - 1)) % SHARDS
    shard_ids = jnp.arange(SHARDS, dtype=jnp.int32)
    lengths = jnp.where(shard_ids == full_shard, CACHE_DEV, lengths)
    lengths = jnp.where(shard_ids == short_shard, CACHE_DEV // 4, lengths)
    return lengths.astype(jnp.int32)


def draw_visible(key, part):
    counts = jax.random.randint(key, (ROWS,), 1, PROMPT + 1)
    ranking = jax.random.permutation(jax.random.fold_in(key, 41), ROWS)
    counts = jnp.where(ranking == 0, PROMPT, counts)
    counts = jnp.where(ranking == 1, 1, counts)
    return counts.astype(jnp.int32)


def shard_levels(key, shape, shards, least, high):
    def one(dim, parts):
        draws = jax.random.uniform(jax.random.fold_in(jax.random.fold_in(key, 6), dim), (parts,), jnp.float32, least / len(shards), high / len(shards))
        return jnp.repeat(jnp.exp(draws), shape[dim] // parts).reshape((-1,) + (1,) * (len(shape) - dim - 1))

    gain = one(*shards[0])
    for cut in shards[1:]:
        gain = gain * one(*cut)
    return gain


def normal_values(stream_key, extent, deviation, bound, shards=(), held_as=jnp.bfloat16):
    values = jax.random.normal(stream_key, extent, jnp.float32) * deviation
    if len(shards) > 0:
        values = shard_levels(stream_key, extent, shards, -0.22, 0.18) * values
    return jnp.clip(values, min=-bound, max=bound).astype(held_as)


def setup_inputs(seed: int = 0) -> dict:
    seeds = jax.random.split(jax.random.key(seed), 12)
    prompt_in = normal_values(seeds[0], (PROMPT, D), 1.0, 6.0, ((1, 8),))
    step_in = normal_values(seeds[1], (STEPS, ROWS, D), 1.0, 6.0, ((2, 8),))
    norm_gain = jnp.clip(1.0 + 0.18 * jax.random.normal(seeds[2], (D,), jnp.float32), 0.099609375, 1.8984375).astype(jnp.bfloat16)
    query_weight = normal_values(seeds[3], (D, KV_HEADS * QPK * HD), (D // 4) ** -0.5, 0.125, ((0, 8), (1, 4)))
    key_weight = normal_values(seeds[4], (D, KV_HEADS * HD), (D // 4) ** -0.5, 0.125, ((0, 8), (1, 4)))
    value_weight = normal_values(seeds[5], (D, KV_HEADS * HD), D ** -0.5, 0.0625, ((0, 8), (1, 4)))
    out_weight = normal_values(seeds[6], (KV_HEADS * QPK * HD, D), (2 * QPK * HD) ** -0.5, 0.125, ((0, 4), (1, 8)))
    key_cache = draw_key_cache(jax.random.fold_in(seeds[11], 71), 0)
    value_cache = draw_value_cache(jax.random.fold_in(seeds[11], 71), 0)
    cache_lengths = draw_cache_lengths(jax.random.fold_in(seeds[11], 71), 0)
    visible = draw_visible(jax.random.fold_in(seeds[11], 71), 0)
    return dict(prompt_in=prompt_in, step_in=step_in, norm_gain=norm_gain, query_weight=query_weight, key_weight=key_weight, value_weight=value_weight, out_weight=out_weight, key_cache=key_cache, value_cache=value_cache, cache_lengths=cache_lengths, visible=visible)


EPSILON = 1e-05

def project(inputs, norm_gain, weight):
    widened = inputs.astype(jnp.float32)
    scaled = (widened * norm_gain.astype(jnp.float32)).astype(jnp.bfloat16)
    inverse = lax.rsqrt(lax.optimization_barrier(jnp.sum(widened * widened, axis=1)) / D + EPSILON)
    product = jnp.dot(scaled, weight, preferred_element_type=jnp.float32)
    return (product * inverse[:, None]).astype(jnp.bfloat16)

def block_partial(queries, key_shard, value_shard, length, extra_keys, extra_values, extra_mask):
    factor = HD ** (-0.5)
    slots_live = jnp.arange(CACHE_DEV, dtype=jnp.int32)[None, :] < length
    cache_scores = jnp.dot(queries, key_shard.T, preferred_element_type=jnp.float32) * factor
    extra_scores = jnp.dot(queries, extra_keys.T, preferred_element_type=jnp.float32) * factor
    cache_scores = jnp.where(slots_live, cache_scores, -jnp.inf)
    extra_scores = jnp.where(extra_mask, extra_scores, -jnp.inf)
    highest = jnp.maximum(lax.optimization_barrier(jnp.max(cache_scores, axis=1)), lax.optimization_barrier(jnp.max(extra_scores, axis=1)))
    cache_weights = jnp.exp(cache_scores - highest[:, None]).astype(jnp.bfloat16)
    extra_weights = jnp.exp(extra_scores - highest[:, None]).astype(jnp.bfloat16)
    totals = lax.optimization_barrier(jnp.sum(cache_weights.astype(jnp.float32), axis=1)) + lax.optimization_barrier(jnp.sum(extra_weights.astype(jnp.float32), axis=1))
    mixture = jnp.dot(cache_weights, value_shard, preferred_element_type=jnp.float32)
    mixture = mixture + jnp.dot(extra_weights, extra_values, preferred_element_type=jnp.float32)
    return (highest, totals, mixture)

def reference(prompt_in, step_in, norm_gain, query_weight, key_weight, value_weight, out_weight, key_cache, value_cache, cache_lengths, visible):
    row_count = PROMPT + STEPS * ROWS
    every_in = jnp.concatenate([prompt_in, step_in.reshape(STEPS * ROWS, D)], axis=0)
    queries = project(every_in, norm_gain, query_weight).reshape(row_count, KV_HEADS, QPK * HD)
    keys = project(every_in, norm_gain, key_weight).reshape(row_count, KV_HEADS, HD)
    values = project(every_in, norm_gain, value_weight).reshape(row_count, KV_HEADS, HD)
    position = jnp.arange(row_count, dtype=jnp.int32)
    is_prompt = position < PROMPT
    after_prompt = jnp.maximum(position - PROMPT, 0)
    row_index = after_prompt % ROWS
    limits = jnp.where(is_prompt, position + 1, visible[row_index])
    owner_rows = jnp.where(is_prompt, -1, row_index)
    owner_steps = jnp.where(is_prompt, -1, after_prompt // ROWS)
    slot_ids = jnp.arange(PROMPT_DEV + ROWS_DEV * STEPS, dtype=jnp.int32)
    slot_prompt = slot_ids < PROMPT_DEV
    decode_slot = jnp.maximum(slot_ids - PROMPT_DEV, 0)

    def per_head(operands):
        head_queries, head_keys, head_values, cache_keys, cache_values = operands
        flat_queries = head_queries.reshape(row_count * QPK, HD)
        prompt_keys = head_keys[:PROMPT]
        prompt_values = head_values[:PROMPT]
        step_keys = head_keys[PROMPT:].reshape(STEPS, ROWS, HD)
        step_values = head_values[PROMPT:].reshape(STEPS, ROWS, HD)

        def per_block(shard_index):
            key_shard = lax.dynamic_slice_in_dim(cache_keys, shard_index * CACHE_DEV, CACHE_DEV, 0)
            value_shard = lax.dynamic_slice_in_dim(cache_values, shard_index * CACHE_DEV, CACHE_DEV, 0)
            block_keys = lax.dynamic_slice_in_dim(prompt_keys, shard_index * PROMPT_DEV, PROMPT_DEV, 0)
            block_values = lax.dynamic_slice_in_dim(prompt_values, shard_index * PROMPT_DEV, PROMPT_DEV, 0)
            own_keys = jnp.swapaxes(lax.dynamic_slice_in_dim(step_keys, shard_index * ROWS_DEV, ROWS_DEV, 1), 0, 1)
            own_values = jnp.swapaxes(lax.dynamic_slice_in_dim(step_values, shard_index * ROWS_DEV, ROWS_DEV, 1), 0, 1)
            extra_keys = jnp.concatenate([block_keys, own_keys.reshape(ROWS_DEV * STEPS, HD)], axis=0)
            extra_values = jnp.concatenate([block_values, own_values.reshape(ROWS_DEV * STEPS, HD)], axis=0)
            seen_prompt = (shard_index * PROMPT_DEV + slot_ids)[None, :] < limits[:, None]
            seen_own = ((shard_index * ROWS_DEV + decode_slot // STEPS)[None, :] == owner_rows[:, None]) & ((decode_slot % STEPS)[None, :] <= owner_steps[:, None])
            seen_keys = jnp.where(slot_prompt[None, :], seen_prompt, seen_own)
            flat_seen = jnp.repeat(seen_keys, QPK, axis=0)
            return block_partial(flat_queries, key_shard, value_shard, cache_lengths[shard_index], extra_keys, extra_values, flat_seen)
        highest, totals, mixture = lax.map(per_block, jnp.arange(SHARDS, dtype=jnp.int32))
        overall = lax.optimization_barrier(jnp.max(highest, axis=0))
        rescale = jnp.exp(highest - overall[None, :])
        summed = lax.optimization_barrier(jnp.sum(mixture * rescale[:, :, None], axis=0))
        denominator = lax.optimization_barrier(jnp.sum(totals * rescale, axis=0))
        result = (summed / denominator[:, None]).astype(jnp.bfloat16)
        return result.reshape(row_count, QPK * HD)
    attended = lax.map(per_head, (jnp.swapaxes(queries, 0, 1), jnp.swapaxes(keys, 0, 1), jnp.swapaxes(values, 0, 1), key_cache, value_cache))
    attended = jnp.swapaxes(attended, 0, 1).reshape(row_count, KV_HEADS * QPK * HD)
    output = jnp.dot(attended, out_weight, preferred_element_type=jnp.float32).astype(jnp.bfloat16)
    return (output[:PROMPT], output[PROMPT:].reshape(STEPS, ROWS, D))
```

```python
import functools

import jax
import jax.numpy as jnp
from jax import lax
from jax.experimental import pallas as pl
from jax.experimental.pallas import tpu as pltpu
from jax.sharding import PartitionSpec as P

HD = 128
EPSILON = 1e-05
MASKED = -1e30
LOG2E = 1.4426950408889634
STAT_ROWS = 16
AT_ONCE = 3
VMEM_BYTES = 50 * 2**20
BF16 = jnp.bfloat16
F32 = jnp.float32


def up(count, multiple):
    return -(-count // multiple) * multiple


def split3(x):
    high = x.astype(BF16).astype(F32)
    rest = x - high
    middle = rest.astype(BF16).astype(F32)
    return high, middle, rest - middle


def column_to_rows(column):
    count = column.shape[0]
    rows = []
    for start in range(0, count, 128):
        size = min(128, count - start)
        part = jnp.broadcast_to(column[start : start + size], (size, 128))
        on = lax.broadcasted_iota(jnp.int32, (size, 128), 0) == lax.broadcasted_iota(
            jnp.int32, (size, 128), 1
        )
        rows.append(jnp.sum(jnp.where(on, part, 0.0), axis=0, keepdims=True))
    return jnp.concatenate(rows, axis=0)


def rows_to_column(rows, index):
    total = 0.0
    for k in range(rows.shape[0]):
        lanes = lax.broadcasted_iota(jnp.int32, (index.shape[0], 128), 1) + 128 * k
        total = total + jnp.sum(
            jnp.where(lanes == index, rows[k : k + 1, :], 0.0), axis=1, keepdims=True
        )
    return total


def stack_stats(rows_list):
    parts = []
    for rows in rows_list:
        parts.extend(split3(rows))
    used = sum(part.shape[0] for part in parts)
    parts.append(jnp.zeros((STAT_ROWS - used, 128), F32))
    return jnp.concatenate(parts, axis=0)


def read_stats(block, count, kinds):
    out = []
    for kind in range(kinds):
        base = kind * 3 * count
        out.append(
            block[base : base + count]
            + block[base + count : base + 2 * count]
            + block[base + 2 * count : base + 3 * count]
        )
    return out


def call(kernel, out_shape, args, name, flops, smem=0, grant=VMEM_BYTES, scratch=()):
    whole = pl.BlockSpec(memory_space=pltpu.VMEM)
    scalar = pl.BlockSpec(memory_space=pltpu.SMEM)
    return pl.pallas_call(
        kernel,
        out_shape=out_shape,
        in_specs=[scalar] * smem + [whole] * (len(args) - smem),
        out_specs=jax.tree.map(lambda _: whole, out_shape),
        scratch_shapes=list(scratch),
        compiler_params=pltpu.CompilerParams(vmem_limit_bytes=grant),
        cost_estimate=pl.CostEstimate(
            flops=int(flops), bytes_accessed=1 << 20, transcendentals=0
        ),
        name=name,
    )(*args)


def shape(rows, columns, dtype, *lead):
    return jax.ShapeDtypeStruct(tuple(lead) + (rows, columns), dtype)


class Sizes:
    def __init__(self, prompt_in, step_in, query_weight, visible, devices, groups):
        self.n = devices
        self.groups = groups
        self.prompt = prompt_in.shape[0]
        self.steps = step_in.shape[0]
        self.row_total = visible.shape[0]
        self.rows = self.prompt + self.steps * self.row_total
        self.width = prompt_in.shape[1]
        self.heads = query_weight.shape[1] // HD
        self.halves = devices // self.heads
        self.piece = self.rows // self.halves
        self.stat_lines = up(self.piece, 128) // 128
        self.square_lines = up(self.rows, 128) // 128
        self.prompt_own = self.prompt // devices
        self.rows_own = self.row_total // devices
        self.decode_own = self.rows_own * self.steps
        self.decode_slots = up(self.decode_own, 16)
        self.prompt_slots = up(self.prompt_own, 16)
        self.slots = self.prompt_slots + self.decode_slots
        self.message = self.piece + STAT_ROWS
        self.project = self.piece + 2 * self.slots + STAT_ROWS


def project_kernel(z, me_ref, xp_ref, xs_ref, gain_ref, wq_ref, wk_ref, wv_ref, even_ref, odd_ref, scaled_ref, kvp_ref, kvd_ref):
    me = me_ref[0]
    gain = gain_ref[...].astype(F32)
    squares = []
    for ref, base, size in (
        (xp_ref, 0, z.prompt),
        (xs_ref, z.prompt, z.steps * z.row_total),
    ):
        wide = ref[...].astype(F32)
        squares.append(jnp.sum(wide * wide, axis=1, keepdims=True))
        scaled_ref[base : base + size, :] = (wide * gain).astype(BF16)
    square_rows = column_to_rows(jnp.concatenate(squares, axis=0))
    pad = jnp.zeros((STAT_ROWS - z.square_lines, 128), F32)
    stats_plain = jnp.concatenate([square_rows, pad], axis=0)
    stats_split = stack_stats([square_rows])
    decode = z.steps * z.row_total
    count = z.n * z.decode_slots
    place = lax.broadcasted_iota(jnp.int32, (count, decode), 0)
    source = lax.broadcasted_iota(jnp.int32, (count, decode), 1)
    slot = place % z.decode_slots
    wanted = (
        (slot // z.rows_own) * z.row_total
        + (place // z.decode_slots) * z.rows_own
        + slot % z.rows_own
    )
    pick = ((wanted == source) & (slot < z.decode_own)).astype(F32).astype(BF16)
    ordered = jnp.dot(
        pick, scaled_ref[z.prompt : z.rows, :], preferred_element_type=F32
    ).astype(BF16)
    for c, ref in enumerate((wk_ref, wv_ref)):
        kvp_ref[:, c * HD : (c + 1) * HD] = jnp.dot(
            scaled_ref[0 : z.prompt, :], ref[...], preferred_element_type=F32
        )
        kvd_ref[:, c * HD : (c + 1) * HD] = jnp.dot(ordered, ref[...], preferred_element_type=F32)
    for d in range(z.n):
        owner = jnp.bitwise_xor(me, d)
        head = owner % z.heads
        half = owner // z.heads
        rows = scaled_ref[pl.ds(pl.multiple_of(half * z.piece, 16), z.piece), :]
        part = jnp.dot(
            rows,
            wq_ref[:, pl.ds(pl.multiple_of(head * HD, HD), HD)],
            preferred_element_type=F32,
        )
        kvp = kvp_ref[pl.ds(pl.multiple_of(owner * z.prompt_own, 8), z.prompt_own), :]
        kvd = kvd_ref[pl.ds(pl.multiple_of(owner * z.decode_slots, 8), z.decode_slots), :]
        ref = odd_ref if d % 2 else even_ref
        stats = stats_split if d % 2 else stats_plain
        everything = jnp.concatenate(
            [part, kvp[:, :HD], kvd[:, :HD], kvp[:, HD:], kvd[:, HD:], stats], axis=0
        )
        ref[d // 2] = everything.astype(ref.dtype)


def pair_sum_kernel(z, even_ref, got_ref, own_ref, *send_refs):
    body = z.project - STAT_ROWS
    for i in range(z.n // 2):
        got = got_ref[i].astype(F32)
        total = even_ref[i, 0:body, :] + got[0:body]
        squares = (
            even_ref[i, body : body + z.square_lines, :]
            + read_stats(got[body:], z.square_lines, 1)[0]
        )
        if i == 0:
            pad = jnp.zeros((STAT_ROWS - z.square_lines, 128), F32)
            own_ref[...] = jnp.concatenate([total, squares, pad], axis=0)
        else:
            send_refs[i - 1][...] = jnp.concatenate(
                [total, stack_stats([squares])], axis=0
            ).astype(BF16)


def finish_kernel(z, features, me_ref, own_ref, *refs):
    got_refs = refs[: z.n // 2 - 1]
    query_ref, key_ref, value_ref = refs[z.n // 2 - 1 :]
    me = me_ref[0]
    body = z.project - STAT_ROWS
    total = own_ref[0:body, :]
    squares = own_ref[body : body + z.square_lines, :]
    for ref in got_refs:
        got = ref[...].astype(F32)
        total = total + got[0:body]
        squares = squares + read_stats(got[body:], z.square_lines, 1)[0]
    inverse = lax.rsqrt(squares / features + EPSILON)
    rows = lax.broadcasted_iota(jnp.int32, (z.piece, 1), 0) + (me // z.heads) * z.piece
    factor = HD ** (-0.5) * LOG2E
    query_ref[...] = (total[0 : z.piece] * (rows_to_column(inverse, rows) * factor)).astype(BF16)
    slot = lax.broadcasted_iota(jnp.int32, (z.slots, 1), 0)
    late = slot - z.prompt_slots
    index = jnp.where(
        slot < z.prompt_slots,
        me * z.prompt_own + slot,
        z.prompt
        + (late // z.rows_own) * z.row_total
        + me * z.rows_own
        + late % z.rows_own,
    )
    own = rows_to_column(inverse, index)
    key_ref[...] = (total[z.piece : z.piece + z.slots] * own).astype(BF16)
    value_ref[...] = (total[z.piece + z.slots : z.piece + 2 * z.slots] * own).astype(BF16)


def attention_kernel(z, pieces, stacked, chunk, me_ref, *refs):
    key_ref, value_ref, bias_ref, extra_key_ref, extra_value_ref, extra_bias_ref = refs[:6]
    query_refs = refs[6 : 6 + len(pieces)]
    out_refs = refs[6 + len(pieces) :]
    me = me_ref[0]
    over = (((1,), (1,)), ((), ()))
    for i, d in enumerate(pieces):
        query = query_refs[i][...]
        half = jnp.bitwise_xor(me, d) // z.heads
        extra_bias = extra_bias_ref[pl.ds(pl.multiple_of(half * z.piece, 8), z.piece), :]
        found = []
        blocks = [
            (key_ref, value_ref, start, chunk) for start in range(0, key_ref.shape[0], chunk)
        ]
        blocks.append((extra_key_ref, extra_value_ref, 0, z.slots))
        for keys, values, start, size in blocks:
            score = lax.dot_general(
                query, keys[start : start + size, :], over, preferred_element_type=F32
            )
            if keys is key_ref:
                score = score + bias_ref[:, start : start + size]
            else:
                score = score + extra_bias
            top = jnp.max(score, axis=1, keepdims=True)
            weight = jnp.exp2(score - top)
            total = jnp.sum(weight, axis=1, keepdims=True)
            mixed = jnp.dot(
                weight.astype(BF16), values[start : start + size, :], preferred_element_type=F32
            )
            found.append((top, total, mixed))
        highest = functools.reduce(jnp.maximum, [top for top, _, _ in found])
        total = 0.0
        mixed = 0.0
        for top, block_total, block_mixed in found:
            scale = jnp.exp2(top - highest)
            total = total + block_total * scale
            mixed = mixed + block_mixed * scale
        stats = stack_stats([column_to_rows(highest), column_to_rows(total)])
        message = jnp.concatenate([mixed, stats], axis=0).astype(BF16)
        if stacked:
            out_refs[0][i] = message
        else:
            out_refs[i][...] = message


def merge(z, messages):
    blocks = []
    for message in messages:
        wide = message.astype(F32)
        top, total = read_stats(wide[z.piece :], z.stat_lines, 2)
        blocks.append((top, total, wide[0 : z.piece]))
    highest = functools.reduce(jnp.maximum, [top for top, _, _ in blocks])
    index = lax.broadcasted_iota(jnp.int32, (z.piece, 1), 0)
    total = 0.0
    mixed = 0.0
    for top, block_total, block_mixed in blocks:
        scale = jnp.exp2(top - highest)
        total = total + block_total * scale
        mixed = mixed + block_mixed * rows_to_column(scale, index)
    return highest, total, mixed


def pair_merge_kernel(z, sets, first_ref, got_first_ref, *refs):
    mine_refs = refs[: len(sets)]
    got_refs = refs[len(sets) : 2 * len(sets)]
    own_ref, *send_refs = refs[2 * len(sets) :]
    places = [(s, k) for s, size in enumerate(sets) for k in range(size)]
    for i in range(z.n // 2):
        if i == 0:
            mine, theirs = first_ref[...], got_first_ref[...]
        else:
            s, k = places[i - 1]
            mine, theirs = mine_refs[s][k], got_refs[s][k]
        highest, total, mixed = merge(z, [mine, theirs])
        message = jnp.concatenate([mixed, stack_stats([highest, total])], axis=0).astype(BF16)
        if i == 0:
            own_ref[...] = message
        else:
            send_refs[i - 1][...] = message


def final_merge_kernel(z, *refs):
    out_ref = refs[-1]
    _, total, mixed = merge(z, [ref[...] for ref in refs[:-1]])
    index = lax.broadcasted_iota(jnp.int32, (z.piece, 1), 0)
    out_ref[...] = (mixed / rows_to_column(total, index)).astype(BF16)


def output_kernel(z, me_ref, weight_ref, *refs):
    piece_refs = refs[: z.n]
    out_refs = refs[z.n : z.n + z.groups]
    sum_ref = refs[-1]
    me = me_ref[0]
    place = me_ref[1]
    columns = weight_ref.shape[1]
    if z.halves > 1:
        sum_ref[...] = jnp.zeros_like(sum_ref)
    total = None
    for d in range(z.n):
        owner = jnp.bitwise_xor(me, d)
        head = owner % z.heads
        product = jnp.dot(
            piece_refs[d][...],
            weight_ref[pl.ds(pl.multiple_of(head * HD, HD), HD), :],
            preferred_element_type=F32,
        )
        if z.halves == 1:
            total = product if total is None else total + product
        else:
            where = pl.ds(pl.multiple_of((owner // z.heads) * z.piece, 8), z.piece)
            sum_ref[where, :] = sum_ref[where, :] + product
    if z.halves == 1:
        sum_ref[...] = total
    prompt_share = z.prompt // z.groups
    step_share = z.row_total // z.groups
    for e in range(z.groups):
        target = jnp.bitwise_xor(place, e)
        rows = [sum_ref[pl.ds(pl.multiple_of(target * prompt_share, 8), prompt_share), :]]
        for s in range(z.steps):
            start = z.prompt + s * z.row_total + target * step_share
            rows.append(sum_ref[pl.ds(pl.multiple_of(start, 8), step_share), :])
        share = jnp.concatenate(rows, axis=0)
        out_refs[e][...] = jnp.concatenate(
            [share[:, : columns // 2], share[:, columns // 2 :]], axis=0
        ).astype(BF16)


def share_sum_kernel(z, *refs):
    prompt_ref, step_ref = refs[z.groups :]
    total = refs[0][...].astype(F32)
    for ref in refs[1 : z.groups]:
        total = total + ref[...].astype(F32)
    prompt_share = z.prompt // z.groups
    step_share = z.row_total // z.groups
    half = total.shape[0] // 2
    columns = total.shape[1]
    for c in range(2):
        rows = total[c * half : (c + 1) * half]
        where = slice(c * columns, (c + 1) * columns)
        prompt_ref[:, where] = rows[0:prompt_share].astype(BF16)
        for s in range(z.steps):
            start = prompt_share + s * step_share
            step_ref[s, :, where] = rows[start : start + step_share].astype(BF16)


def swap(x, axis, size, d):
    return lax.ppermute(x, axis, [(i, i ^ d) for i in range(size)])


def on_device(
    prompt_in,
    step_in,
    norm_gain,
    query_weight,
    key_weight,
    value_weight,
    out_weight,
    key_cache,
    value_cache,
    cache_lengths,
    visible,
):
    n = lax.axis_size("ctx")
    groups = lax.axis_size("kv")
    z = Sizes(prompt_in, step_in, query_weight, visible, n, groups)
    me = lax.axis_index("ctx").astype(jnp.int32)
    place = lax.axis_index("kv").astype(jnp.int32)
    where = jnp.stack([me, place])
    pairs = n // 2

    row = jnp.arange(z.rows, dtype=jnp.int32)
    is_prompt = row < z.prompt
    late = jnp.maximum(row - z.prompt, 0)
    limit = jnp.where(is_prompt, row + 1, visible[late % z.row_total])
    slot = jnp.arange(z.slots, dtype=jnp.int32)
    late_slot = jnp.maximum(slot - z.prompt_slots, 0)
    seen_prompt = (slot < z.prompt_own) & ((me * z.prompt_own + slot) < limit[:, None])
    seen_own = (
        (slot >= z.prompt_slots)
        & (late_slot < z.decode_own)
        & ~is_prompt[:, None]
        & ((me * z.rows_own + late_slot % z.rows_own) == (late % z.row_total)[:, None])
        & ((late_slot // z.rows_own) <= (late // z.row_total)[:, None])
    )
    extra_bias = jnp.where(seen_prompt | seen_own, 0.0, MASKED).astype(F32)
    cache_slots = key_cache.shape[1]
    live = lax.broadcasted_iota(jnp.int32, (1, cache_slots), 1) < cache_lengths[0]
    bias = jnp.where(live, 0.0, MASKED).astype(F32)

    even, odd = call(
        functools.partial(project_kernel, z),
        [shape(z.project, HD, F32, pairs), shape(z.project, HD, BF16, pairs)],
        (
            where,
            prompt_in,
            step_in.reshape(z.steps * z.row_total, z.width),
            norm_gain.reshape(1, z.width),
            query_weight,
            key_weight,
            value_weight,
        ),
        "project",
        2 * z.rows * z.width * (z.heads + 2) * HD,
        smem=1,
        scratch=[
            pltpu.VMEM((z.rows, z.width), BF16),
            pltpu.VMEM((z.prompt, 2 * HD), F32),
            pltpu.VMEM((z.n * z.decode_slots, 2 * HD), F32),
        ],
    )
    got = swap(odd, "ctx", n, 1)
    own, *sends = call(
        functools.partial(pair_sum_kernel, z),
        [shape(z.project, HD, F32)] + [shape(z.project, HD, BF16)] * (pairs - 1),
        (even, got),
        "pair_sum",
        1e6,
    )
    gots = [swap(send, "ctx", n, 2 * (i + 1)) for i, send in enumerate(sends)]
    query, extra_key, extra_value = call(
        functools.partial(finish_kernel, z, z.width * n),
        [shape(z.piece, HD, BF16), shape(z.slots, HD, BF16), shape(z.slots, HD, BF16)],
        (where, own, *gots),
        "finish",
        1e6,
        smem=1,
    )

    queries = {0: query}
    for i in range(1, pairs):
        queries[2 * i] = swap(query, "ctx", n, 2 * i)
    queries[1] = swap(query, "ctx", n, 1)
    for i in range(1, pairs):
        queries[2 * i + 1] = swap(queries[2 * i], "ctx", n, 1)

    def attend(pieces, stacked, name):
        message = shape(z.message, HD, BF16)
        outs = [shape(z.message, HD, BF16, len(pieces))] if stacked else [message] * len(pieces)
        chunk = 1024 if cache_slots % 1024 == 0 else cache_slots
        return call(
            functools.partial(attention_kernel, z, pieces, stacked, chunk),
            outs,
            (where, key_cache[0], value_cache[0], bias, extra_key, extra_value, extra_bias)
            + tuple(queries[d] for d in pieces),
            name,
            8 * len(pieces) * z.piece * cache_slots * HD,
            smem=1,
        )

    first, first_odd = attend((0, 1), False, "attend_chip")
    odd = list(range(3, n, 2))
    sets = [tuple(odd[k : k + AT_ONCE]) for k in range(0, len(odd), AT_ONCE)]
    rest_odd = [attend(pieces, True, f"attend_odd{k}")[0] for k, pieces in enumerate(sets)]
    got_first = swap(first_odd, "ctx", n, 1)
    got_rest = [swap(block, "ctx", n, 1) for block in rest_odd]
    rest = [
        attend(tuple(d - 1 for d in pieces), True, f"attend_even{k}")[0]
        for k, pieces in enumerate(sets)
    ]

    message = shape(z.message, HD, BF16)
    own, *sends = call(
        functools.partial(pair_merge_kernel, z, [len(pieces) for pieces in sets]),
        [message] * pairs,
        (first, got_first, *rest, *got_rest),
        "pair_merge",
        1e6,
    )
    gots = [swap(send, "ctx", n, 2 * (i + 1)) for i, send in enumerate(sends)]
    (attended,) = call(
        functools.partial(final_merge_kernel, z),
        [shape(z.piece, HD, BF16)],
        (own, *gots),
        "final_merge",
        1e6,
    )
    heads = {0: attended}
    for i in range(1, pairs):
        heads[2 * i] = swap(attended, "ctx", n, 2 * i)
    heads[1] = swap(attended, "ctx", n, 1)
    for i in range(1, pairs):
        heads[2 * i + 1] = swap(heads[2 * i], "ctx", n, 1)

    columns = out_weight.shape[1]
    share_rows = 2 * z.rows // groups
    shares = call(
        functools.partial(output_kernel, z),
        [shape(share_rows, columns // 2, BF16)] * groups,
        (where, out_weight) + tuple(heads[d] for d in range(n)),
        "output",
        2 * z.rows * z.heads * HD * columns,
        smem=1,
        scratch=[pltpu.VMEM((z.rows, columns), F32)],
    )
    shares = [shares[0]] + [swap(shares[e], "kv", groups, e) for e in range(1, groups)]
    prompt_out, step_out = call(
        functools.partial(share_sum_kernel, z),
        [
            shape(z.prompt // groups, columns, BF16),
            shape(z.row_total // groups, columns, BF16, z.steps),
        ],
        tuple(shares),
        "share_sum",
        1e6,
    )
    return (prompt_out, step_out)


def solution(mesh):
    placed = (
        P(None, "ctx"),
        P(None, None, "ctx"),
        P("ctx"),
        P("ctx", "kv"),
        P("ctx", "kv"),
        P("ctx", "kv"),
        P("kv", "ctx"),
        P("kv", "ctx", None),
        P("kv", "ctx", None),
        P("ctx"),
        P(),
    )
    return jax.shard_map(
        on_device,
        mesh=mesh,
        in_specs=placed,
        out_specs=(P("kv", "ctx"), P(None, "kv", "ctx")),
        check_vma=False,
    )
```

```python
import functools

import jax
import jax.numpy as jnp
from jax import lax
from jax.experimental import pallas as pl
from jax.experimental.pallas import tpu as pltpu
from jax.sharding import PartitionSpec as P

HD = 128
EPSILON = 1e-05
MASKED = -1e30
LOG2E = 1.4426950408889634
STAT_ROWS = 16
AT_ONCE = 3
VMEM_BYTES = 20 * 2**20
BF16 = jnp.bfloat16
F32 = jnp.float32


def up(count, multiple):
    return -(-count // multiple) * multiple


def split3(x):
    high = x.astype(BF16).astype(F32)
    rest = x - high
    middle = rest.astype(BF16).astype(F32)
    return high, middle, rest - middle


def column_to_rows(column):
    count = column.shape[0]
    rows = []
    for start in range(0, count, 128):
        size = min(128, count - start)
        part = jnp.broadcast_to(column[start : start + size], (size, 128))
        on = lax.broadcasted_iota(jnp.int32, (size, 128), 0) == lax.broadcasted_iota(
            jnp.int32, (size, 128), 1
        )
        rows.append(jnp.sum(jnp.where(on, part, 0.0), axis=0, keepdims=True))
    return jnp.concatenate(rows, axis=0)


def rows_to_column(rows, index):
    total = 0.0
    for k in range(rows.shape[0]):
        lanes = lax.broadcasted_iota(jnp.int32, (index.shape[0], 128), 1) + 128 * k
        total = total + jnp.sum(
            jnp.where(lanes == index, rows[k : k + 1, :], 0.0), axis=1, keepdims=True
        )
    return total


def stack_stats(rows_list):
    parts = []
    for rows in rows_list:
        parts.extend(split3(rows))
    used = sum(part.shape[0] for part in parts)
    parts.append(jnp.zeros((STAT_ROWS - used, 128), F32))
    return jnp.concatenate(parts, axis=0)


def read_stats(block, count, kinds):
    out = []
    for kind in range(kinds):
        base = kind * 3 * count
        out.append(
            block[base : base + count]
            + block[base + count : base + 2 * count]
            + block[base + 2 * count : base + 3 * count]
        )
    return out


def call(kernel, out_shape, args, name, flops, smem=0, far=0, grant=VMEM_BYTES, scratch=()):
    whole = pl.BlockSpec(memory_space=pltpu.VMEM)
    scalar = pl.BlockSpec(memory_space=pltpu.SMEM)
    return pl.pallas_call(
        kernel,
        out_shape=out_shape,
        in_specs=[scalar] * smem
        + [whole] * (len(args) - smem - far)
        + [pl.BlockSpec(memory_space=pltpu.HBM)] * far,
        out_specs=jax.tree.map(lambda _: whole, out_shape),
        scratch_shapes=list(scratch),
        compiler_params=pltpu.CompilerParams(vmem_limit_bytes=grant),
        cost_estimate=pl.CostEstimate(
            flops=int(flops), bytes_accessed=1 << 20, transcendentals=0
        ),
        name=name,
    )(*args)


def shape(rows, columns, dtype, *lead):
    return jax.ShapeDtypeStruct(tuple(lead) + (rows, columns), dtype)


class Sizes:
    def __init__(self, prompt_in, step_in, query_weight, visible, devices, groups):
        self.n = devices
        self.groups = groups
        self.prompt = prompt_in.shape[0]
        self.steps = step_in.shape[0]
        self.row_total = visible.shape[0]
        self.rows = self.prompt + self.steps * self.row_total
        self.width = prompt_in.shape[1]
        self.heads = query_weight.shape[1] // HD
        self.halves = devices // self.heads
        self.piece = self.rows // self.halves
        self.stat_lines = up(self.piece, 128) // 128
        self.square_lines = up(self.rows, 128) // 128
        self.prompt_own = self.prompt // devices
        self.rows_own = self.row_total // devices
        self.decode_own = self.rows_own * self.steps
        self.decode_slots = up(self.decode_own, 16)
        self.prompt_slots = up(self.prompt_own, 16)
        self.slots = self.prompt_slots + self.decode_slots
        self.message = self.piece + STAT_ROWS
        self.project = self.piece + 2 * self.slots + STAT_ROWS


def project_kernel(z, gain_ref, xp_hbm, xs_hbm, wq_hbm, wk_hbm, wv_hbm, even_ref, odd_ref, xp_ref, xs_ref, wq_ref, wk_ref, wv_ref, scaled_ref, query_ref, kvp_ref, kvd_ref, sems):
    me = lax.axis_index("ctx")
    depth = z.width // 2
    loads = [
        pltpu.make_async_copy(xp_hbm, xp_ref, sems.at[0]),
        pltpu.make_async_copy(xs_hbm, xs_ref, sems.at[1]),
        pltpu.make_async_copy(wk_hbm, wk_ref, sems.at[2]),
        pltpu.make_async_copy(wv_hbm, wv_ref, sems.at[3]),
    ]
    loads += [
        pltpu.make_async_copy(wq_hbm.at[pl.ds(k * depth, depth), :], wq_ref.at[k], sems.at[4 + k])
        for k in range(2)
    ]
    for load in loads:
        load.start()
    gain = gain_ref[...].astype(F32)
    gain = jnp.concatenate([gain[k : k + 1, :] for k in range(gain.shape[0])], axis=1)
    squares = []
    for k, (ref, base, size) in enumerate(
        (
            (xp_ref, 0, z.prompt),
            (xs_ref, z.prompt, z.steps * z.row_total),
        )
    ):
        loads[k].wait()
        wide = ref[...].astype(F32)
        squares.append(jnp.sum(wide * wide, axis=1, keepdims=True))
        scaled_ref[base : base + size, :] = (wide * gain).astype(BF16)
    square_rows = column_to_rows(jnp.concatenate(squares, axis=0))
    pad = jnp.zeros((STAT_ROWS - z.square_lines, 128), F32)
    stats_plain = jnp.concatenate([square_rows, pad], axis=0)
    stats_split = stack_stats([square_rows])
    decode = z.steps * z.row_total
    count = z.n * z.decode_slots
    place = lax.broadcasted_iota(jnp.int32, (count, decode), 0)
    source = lax.broadcasted_iota(jnp.int32, (count, decode), 1)
    slot = place % z.decode_slots
    wanted = (
        (slot // z.rows_own) * z.row_total
        + (place // z.decode_slots) * z.rows_own
        + slot % z.rows_own
    )
    pick = ((wanted == source) & (slot < z.decode_own)).astype(F32).astype(BF16)
    ordered = jnp.dot(
        pick, scaled_ref[z.prompt : z.rows, :], preferred_element_type=F32
    ).astype(BF16)
    for c, ref in enumerate((wk_ref, wv_ref)):
        loads[2 + c].wait()
        kvp_ref[:, c * HD : (c + 1) * HD] = jnp.dot(
            scaled_ref[0 : z.prompt, :], ref[...], preferred_element_type=F32
        )
        kvd_ref[:, c * HD : (c + 1) * HD] = jnp.dot(ordered, ref[...], preferred_element_type=F32)
    loads[4].wait()
    product = jnp.dot(scaled_ref[:, :depth], wq_ref[0], preferred_element_type=F32)
    loads[5].wait()
    query_ref[...] = product + jnp.dot(
        scaled_ref[:, depth:], wq_ref[1], preferred_element_type=F32
    )
    for d in range(z.n):
        owner = jnp.bitwise_xor(me, d)
        half = owner // z.heads
        part = query_ref[
            pl.ds(pl.multiple_of(half * z.piece, 8), z.piece),
            pl.ds(pl.multiple_of(owner % z.heads * HD, HD), HD),
        ]
        kvp = kvp_ref[pl.ds(pl.multiple_of(owner * z.prompt_own, 8), z.prompt_own), :]
        kvd = kvd_ref[pl.ds(pl.multiple_of(owner * z.decode_slots, 8), z.decode_slots), :]
        ref = odd_ref if d % 2 else even_ref
        stats = stats_split if d % 2 else stats_plain
        everything = jnp.concatenate(
            [part, kvp[:, :HD], kvd[:, :HD], kvp[:, HD:], kvd[:, HD:], stats], axis=0
        )
        ref[d // 2] = everything.astype(ref.dtype)


def pair_sum_kernel(z, even_ref, got_ref, own_ref, *send_refs):
    body = z.project - STAT_ROWS
    for i in range(z.n // 2):
        got = got_ref[i].astype(F32)
        total = even_ref[i, 0:body, :] + got[0:body]
        squares = (
            even_ref[i, body : body + z.square_lines, :]
            + read_stats(got[body:], z.square_lines, 1)[0]
        )
        if i == 0:
            pad = jnp.zeros((STAT_ROWS - z.square_lines, 128), F32)
            own_ref[...] = jnp.concatenate([total, squares, pad], axis=0)
        else:
            send_refs[i - 1][...] = jnp.concatenate(
                [total, stack_stats([squares])], axis=0
            ).astype(BF16)


def finish_kernel(z, features, own_ref, *refs):
    got_refs = refs[: z.n // 2 - 1]
    query_ref, key_ref, value_ref = refs[z.n // 2 - 1 :]
    me = lax.axis_index("ctx")
    body = z.project - STAT_ROWS
    total = own_ref[0:body, :]
    squares = own_ref[body : body + z.square_lines, :]
    for ref in got_refs:
        got = ref[...].astype(F32)
        total = total + got[0:body]
        squares = squares + read_stats(got[body:], z.square_lines, 1)[0]
    inverse = lax.rsqrt(squares / features + EPSILON)
    rows = lax.broadcasted_iota(jnp.int32, (z.piece, 1), 0) + (me // z.heads) * z.piece
    factor = HD ** (-0.5) * LOG2E
    query_ref[...] = (total[0 : z.piece] * (rows_to_column(inverse, rows) * factor)).astype(BF16)
    slot = lax.broadcasted_iota(jnp.int32, (z.slots, 1), 0)
    late = slot - z.prompt_slots
    index = jnp.where(
        slot < z.prompt_slots,
        me * z.prompt_own + slot,
        z.prompt
        + (late // z.rows_own) * z.row_total
        + me * z.rows_own
        + late % z.rows_own,
    )
    own = rows_to_column(inverse, index)
    key_ref[...] = (total[z.piece : z.piece + z.slots] * own).astype(BF16)
    value_ref[...] = (total[z.piece + z.slots : z.piece + 2 * z.slots] * own).astype(BF16)


def mask_kernel(z, length_ref, visible_ref, bias_ref, extra_ref):
    me = lax.axis_index("ctx")
    live = lax.broadcasted_iota(jnp.int32, bias_ref.shape, 1) < length_ref[0]
    bias_ref[...] = jnp.where(live, 0.0, MASKED)
    row = lax.broadcasted_iota(jnp.int32, (z.rows, 1), 0)
    late = row - z.prompt
    step = late // z.row_total
    place = late - step * z.row_total
    lanes = lax.broadcasted_iota(jnp.int32, (z.rows, z.row_total), 1)
    allowed = jnp.sum(
        jnp.where(lanes == place, visible_ref[...].astype(F32), 0.0), axis=1, keepdims=True
    )
    limit = jnp.where(late < 0, row + 1, allowed.astype(jnp.int32))
    slot = lax.broadcasted_iota(jnp.int32, (z.rows, z.slots), 1)
    late_slot = slot - z.prompt_slots
    from_prompt = (slot < z.prompt_own) & (me * z.prompt_own + slot < limit)
    from_decode = (
        (late_slot >= 0)
        & (late_slot < z.decode_own)
        & (late >= 0)
        & (me * z.rows_own + late_slot % z.rows_own == place)
        & (late_slot // z.rows_own <= step)
    )
    extra_ref[...] = jnp.where(from_prompt | from_decode, 0.0, MASKED)


def attention_kernel(z, pieces, stacked, chunk, *refs):
    key_ref, value_ref, bias_ref, extra_key_ref, extra_value_ref, extra_bias_ref = refs[:6]
    query_refs = refs[6 : 6 + len(pieces)]
    out_refs = refs[6 + len(pieces) :]
    me = lax.axis_index("ctx")
    over = (((1,), (1,)), ((), ()))
    for i, d in enumerate(pieces):
        query = query_refs[i][...]
        half = jnp.bitwise_xor(me, d) // z.heads
        extra_bias = extra_bias_ref[pl.ds(pl.multiple_of(half * z.piece, 8), z.piece), :]
        found = []
        blocks = [
            (key_ref, value_ref, start, chunk) for start in range(0, key_ref.shape[0], chunk)
        ]
        blocks.append((extra_key_ref, extra_value_ref, 0, z.slots))
        for keys, values, start, size in blocks:
            score = lax.dot_general(
                query, keys[start : start + size, :], over, preferred_element_type=F32
            )
            if keys is key_ref:
                score = score + bias_ref[:, start : start + size]
            else:
                score = score + extra_bias
            top = jnp.max(score, axis=1, keepdims=True)
            weight = jnp.exp2(score - top).astype(BF16)
            beside = jnp.concatenate(
                [values[start : start + size, :], jnp.ones((size, HD), BF16)], axis=1
            )
            found.append((top, jnp.dot(weight, beside, preferred_element_type=F32)))
        highest = functools.reduce(jnp.maximum, [top for top, _ in found])
        mixed = 0.0
        for top, block in found:
            mixed = mixed + block * jnp.exp2(top - highest)
        stats = stack_stats([column_to_rows(highest), column_to_rows(mixed[:, HD : HD + 1])])
        message = jnp.concatenate([mixed[:, :HD], stats], axis=0).astype(BF16)
        if stacked:
            out_refs[0][i] = message
        else:
            out_refs[i][...] = message


def merge(z, messages):
    blocks = []
    for message in messages:
        wide = message.astype(F32)
        top, total = read_stats(wide[z.piece :], z.stat_lines, 2)
        blocks.append((top, total, wide[0 : z.piece]))
    highest = functools.reduce(jnp.maximum, [top for top, _, _ in blocks])
    index = lax.broadcasted_iota(jnp.int32, (z.piece, 1), 0)
    total = 0.0
    mixed = 0.0
    for top, block_total, block_mixed in blocks:
        scale = jnp.exp2(top - highest)
        total = total + block_total * scale
        mixed = mixed + block_mixed * rows_to_column(scale, index)
    return highest, total, mixed


def pair_merge_kernel(z, sets, *refs):
    mine_refs = refs[: len(sets)]
    got_refs = refs[len(sets) : 2 * len(sets)]
    send_refs = refs[2 * len(sets) :]
    places = [(s, k) for s, size in enumerate(sets) for k in range(size)]
    for send_ref, (s, k) in zip(send_refs, places):
        highest, total, mixed = merge(z, [mine_refs[s][k], got_refs[s][k]])
        send_ref[...] = jnp.concatenate([mixed, stack_stats([highest, total])], axis=0).astype(BF16)


def final_merge_kernel(z, *refs):
    out_ref = refs[-1]
    _, total, mixed = merge(z, [ref[...] for ref in refs[:-1]])
    index = lax.broadcasted_iota(jnp.int32, (z.piece, 1), 0)
    out_ref[...] = (mixed / rows_to_column(total, index)).astype(BF16)


def output_kernel(z, weight_ref, *refs):
    piece_refs = refs[: z.n]
    out_refs = refs[z.n : z.n + z.groups]
    sum_ref = refs[-1]
    me = lax.axis_index("ctx")
    place = lax.axis_index("kv")
    columns = weight_ref.shape[1]
    if z.halves > 1:
        sum_ref[...] = jnp.zeros_like(sum_ref)
    total = None
    swapped = me % 2 == 1
    for d in range(0, z.n, 2):
        owner = jnp.bitwise_xor(me, d)
        first, second = piece_refs[d][...], piece_refs[d + 1][...]
        both = jnp.where(
            swapped,
            jnp.concatenate([second, first], axis=1),
            jnp.concatenate([first, second], axis=1),
        )
        product = jnp.dot(
            both,
            weight_ref[pl.ds(pl.multiple_of(owner % z.heads // 2 * 2 * HD, 2 * HD), 2 * HD), :],
            preferred_element_type=F32,
        )
        if z.halves == 1:
            total = product if total is None else total + product
        else:
            where = pl.ds(pl.multiple_of((owner // z.heads) * z.piece, 8), z.piece)
            sum_ref[where, :] = sum_ref[where, :] + product
    if z.halves == 1:
        sum_ref[...] = total
    prompt_share = z.prompt // z.groups
    step_share = z.row_total // z.groups
    for e in range(z.groups):
        target = jnp.bitwise_xor(place, e)
        rows = [sum_ref[pl.ds(pl.multiple_of(target * prompt_share, 8), prompt_share), :]]
        for s in range(z.steps):
            start = z.prompt + s * z.row_total + target * step_share
            rows.append(sum_ref[pl.ds(pl.multiple_of(start, 8), step_share), :])
        share = jnp.concatenate(rows, axis=0)
        out_refs[e][...] = jnp.concatenate(
            [share[:, : columns // 2], share[:, columns // 2 :]], axis=0
        ).astype(BF16)


def share_sum_kernel(z, *refs):
    prompt_ref, step_ref = refs[z.groups :]
    total = refs[0][...].astype(F32)
    for ref in refs[1 : z.groups]:
        total = total + ref[...].astype(F32)
    prompt_share = z.prompt // z.groups
    step_share = z.row_total // z.groups
    half = total.shape[0] // 2
    columns = total.shape[1]
    for c in range(2):
        rows = total[c * half : (c + 1) * half]
        where = slice(c * columns, (c + 1) * columns)
        prompt_ref[:, where] = rows[0:prompt_share].astype(BF16)
        for s in range(z.steps):
            start = prompt_share + s * step_share
            step_ref[s, :, where] = rows[start : start + step_share].astype(BF16)


def swap(x, axis, size, d):
    return lax.ppermute(x, axis, [(i, i ^ d) for i in range(size)])


def on_device(
    prompt_in,
    step_in,
    norm_gain,
    query_weight,
    key_weight,
    value_weight,
    out_weight,
    key_cache,
    value_cache,
    cache_lengths,
    visible,
):
    n = lax.axis_size("ctx")
    groups = lax.axis_size("kv")
    z = Sizes(prompt_in, step_in, query_weight, visible, n, groups)
    pairs = n // 2

    cache_slots = key_cache.shape[1]
    def masks(lengths, seen):
        return call(
            functools.partial(mask_kernel, z),
            [shape(1, cache_slots, F32), shape(z.rows, z.slots, F32)],
            (lengths, seen.reshape(1, z.row_total)),
            "masks",
            1e6,
            smem=1,
        )

    even, odd = call(
        functools.partial(project_kernel, z),
        [shape(z.project, HD, F32, pairs), shape(z.project, HD, BF16, pairs)],
        (
            norm_gain.reshape(z.width // 128, 128),
            prompt_in,
            step_in.reshape(z.steps * z.row_total, z.width),
            query_weight,
            key_weight,
            value_weight,
        ),
        "project",
        2 * z.rows * z.width * (z.heads + 2) * HD,
        far=5,
        scratch=[
            pltpu.VMEM((z.prompt, z.width), BF16),
            pltpu.VMEM((z.steps * z.row_total, z.width), BF16),
            pltpu.VMEM((2, z.width // 2, z.heads * HD), BF16),
            pltpu.VMEM((z.width, HD), BF16),
            pltpu.VMEM((z.width, HD), BF16),
            pltpu.VMEM((z.rows, z.width), BF16),
            pltpu.VMEM((z.rows, z.heads * HD), F32),
            pltpu.VMEM((z.prompt, 2 * HD), F32),
            pltpu.VMEM((z.n * z.decode_slots, 2 * HD), F32),
            pltpu.SemaphoreType.DMA((6,)),
        ],
    )
    got = swap(odd, "ctx", n, 1)
    own, *sends = call(
        functools.partial(pair_sum_kernel, z),
        [shape(z.project, HD, F32)] + [shape(z.project, HD, BF16)] * (pairs - 1),
        (even, got),
        "pair_sum",
        1e6,
    )
    visible, *sends = lax.optimization_barrier((visible, *sends))
    gots = [swap(send, "ctx", n, 2 * (i + 1)) for i, send in enumerate(sends)]
    bias, extra_bias = masks(cache_lengths, visible)
    own, bias, extra_bias = lax.optimization_barrier((own, bias, extra_bias))
    query, extra_key, extra_value = call(
        functools.partial(finish_kernel, z, z.width * n),
        [shape(z.piece, HD, BF16), shape(z.slots, HD, BF16), shape(z.slots, HD, BF16)],
        (own, *gots),
        "finish",
        1e6,
    )

    queries = {1: swap(query, "ctx", n, 1)}
    for i in range(1, pairs):
        queries[2 * i] = swap(query, "ctx", n, 2 * i)

    def attend(pieces, stacked, name):
        message = shape(z.message, HD, BF16)
        outs = [shape(z.message, HD, BF16, len(pieces))] if stacked else [message] * len(pieces)
        chunk = 1024 if cache_slots % 1024 == 0 else cache_slots
        return call(
            functools.partial(attention_kernel, z, pieces, stacked, chunk),
            outs,
            (key_cache[0], value_cache[0], bias, extra_key, extra_value, extra_bias)
            + tuple(queries[d] for d in pieces),
            name,
            8 * len(pieces) * z.piece * cache_slots * HD,
            )

    (first_odd,) = attend((1,), False, "attend_core")
    first_odd, *passed = lax.optimization_barrier(
        (first_odd, *[queries[2 * i] for i in range(1, pairs)])
    )
    for i in range(1, pairs):
        queries[2 * i] = passed[i - 1]
        queries[2 * i + 1] = swap(queries[2 * i], "ctx", n, 1)
    odd = list(range(3, n, 2))
    sets = [tuple(odd[k : k + AT_ONCE]) for k in range(0, len(odd), AT_ONCE)]
    rest_odd = [attend(pieces, True, f"attend_odd{k}")[0] for k, pieces in enumerate(sets)]
    got_first = swap(first_odd, "ctx", n, 1)
    got_rest = [swap(block, "ctx", n, 1) for block in rest_odd]
    rest = [
        attend(tuple(d - 1 for d in pieces), True, f"attend_even{k}")[0]
        for k, pieces in enumerate(sets)
    ]

    message = shape(z.message, HD, BF16)
    sends = call(
        functools.partial(pair_merge_kernel, z, [len(pieces) for pieces in sets]),
        [message] * (pairs - 1),
        (*rest, *got_rest),
        "pair_merge",
        1e6,
    )
    query, *sends = lax.optimization_barrier((query, *sends))
    gots = [swap(send, "ctx", n, 2 * (i + 1)) for i, send in enumerate(sends)]
    queries[0] = query
    (own,) = attend((0,), False, "attend_own")
    (attended,) = call(
        functools.partial(final_merge_kernel, z),
        [shape(z.piece, HD, BF16)],
        (own, got_first, *gots),
        "final_merge",
        1e6,
    )
    heads = {0: attended}
    for i in range(1, pairs):
        heads[2 * i] = swap(attended, "ctx", n, 2 * i)
    heads[1] = swap(attended, "ctx", n, 1)
    for i in range(1, pairs):
        heads[2 * i + 1] = swap(heads[2 * i], "ctx", n, 1)

    columns = out_weight.shape[1]
    share_rows = 2 * z.rows // groups
    shares = call(
        functools.partial(output_kernel, z),
        [shape(share_rows, columns // 2, BF16)] * groups,
        (out_weight,) + tuple(heads[d] for d in range(n)),
        "output",
        2 * z.rows * z.heads * HD * columns,
        scratch=[pltpu.VMEM((z.rows, columns), F32)],
    )
    shares = [shares[0]] + [swap(shares[e], "kv", groups, e) for e in range(1, groups)]
    prompt_out, step_out = call(
        functools.partial(share_sum_kernel, z),
        [
            shape(z.prompt // groups, columns, BF16),
            shape(z.row_total // groups, columns, BF16, z.steps),
        ],
        tuple(shares),
        "share_sum",
        1e6,
    )
    return (prompt_out, step_out)


def solution(mesh):
    placed = (
        P(None, "ctx"),
        P(None, None, "ctx"),
        P("ctx"),
        P("ctx", "kv"),
        P("ctx", "kv"),
        P("ctx", "kv"),
        P("kv", "ctx"),
        P("kv", "ctx", None),
        P("kv", "ctx", None),
        P("ctx"),
        P(),
    )
    return jax.shard_map(
        on_device,
        mesh=mesh,
        in_specs=placed,
        out_specs=(P("kv", "ctx"), P(None, "kv", "ctx")),
        check_vma=False,
    )
```

```python
import functools

import jax
import jax.numpy as jnp
from jax import lax
from jax.experimental import pallas as pl
from jax.experimental.pallas import tpu as pltpu
from jax.sharding import PartitionSpec as P

HD = 128
EPSILON = 1e-05
MASKED = -1e30
LOG2E = 1.4426950408889634
STAT_ROWS = 16
AT_ONCE = 3
VMEM_BYTES = 20 * 2**20
BF16 = jnp.bfloat16
F32 = jnp.float32


def up(count, multiple):
    return -(-count // multiple) * multiple


def split3(x):
    high = x.astype(BF16).astype(F32)
    rest = x - high
    middle = rest.astype(BF16).astype(F32)
    return high, middle, rest - middle


def column_to_rows(column):
    count = column.shape[0]
    rows = []
    for start in range(0, count, 128):
        size = min(128, count - start)
        part = jnp.broadcast_to(column[start : start + size], (size, 128))
        on = lax.broadcasted_iota(jnp.int32, (size, 128), 0) == lax.broadcasted_iota(
            jnp.int32, (size, 128), 1
        )
        rows.append(jnp.sum(jnp.where(on, part, 0.0), axis=0, keepdims=True))
    return jnp.concatenate(rows, axis=0)


def rows_to_column(rows, index):
    total = 0.0
    for k in range(rows.shape[0]):
        lanes = lax.broadcasted_iota(jnp.int32, (index.shape[0], 128), 1) + 128 * k
        total = total + jnp.sum(
            jnp.where(lanes == index, rows[k : k + 1, :], 0.0), axis=1, keepdims=True
        )
    return total


def stack_stats(rows_list):
    parts = []
    for rows in rows_list:
        parts.extend(split3(rows))
    used = sum(part.shape[0] for part in parts)
    parts.append(jnp.zeros((STAT_ROWS - used, 128), F32))
    return jnp.concatenate(parts, axis=0)


def read_stats(block, count, kinds):
    out = []
    for kind in range(kinds):
        base = kind * 3 * count
        out.append(
            block[base : base + count]
            + block[base + count : base + 2 * count]
            + block[base + 2 * count : base + 3 * count]
        )
    return out


def call(kernel, out_shape, args, name, flops, smem=0, far=0, grant=VMEM_BYTES, scratch=()):
    whole = pl.BlockSpec(memory_space=pltpu.VMEM)
    scalar = pl.BlockSpec(memory_space=pltpu.SMEM)
    near = len(args) - far
    args = args[:near] + tuple(
        pltpu.with_memory_space_constraint(x, pltpu.HBM) for x in args[near:]
    )
    return pl.pallas_call(
        kernel,
        out_shape=out_shape,
        in_specs=[scalar] * smem
        + [whole] * (near - smem)
        + [pl.BlockSpec(memory_space=pltpu.HBM)] * far,
        out_specs=jax.tree.map(lambda _: whole, out_shape),
        scratch_shapes=list(scratch),
        compiler_params=pltpu.CompilerParams(vmem_limit_bytes=grant),
        cost_estimate=pl.CostEstimate(
            flops=int(flops), bytes_accessed=1 << 20, transcendentals=0
        ),
        name=name,
    )(*args)


def shape(rows, columns, dtype, *lead):
    return jax.ShapeDtypeStruct(tuple(lead) + (rows, columns), dtype)


class Sizes:
    def __init__(self, prompt_in, step_in, query_weight, visible, devices, groups):
        self.n = devices
        self.groups = groups
        self.prompt = prompt_in.shape[0]
        self.steps = step_in.shape[0]
        self.row_total = visible.shape[0]
        self.rows = self.prompt + self.steps * self.row_total
        self.width = prompt_in.shape[1]
        self.heads = query_weight.shape[1] // HD
        self.halves = devices // self.heads
        self.piece = self.rows // self.halves
        self.stat_lines = up(self.piece, 128) // 128
        self.square_lines = up(self.rows, 128) // 128
        self.prompt_own = self.prompt // devices
        self.rows_own = self.row_total // devices
        self.decode_own = self.rows_own * self.steps
        self.decode_slots = up(self.decode_own, 16)
        self.prompt_slots = up(self.prompt_own, 16)
        self.slots = self.prompt_slots + self.decode_slots
        self.message = self.piece + STAT_ROWS
        self.project = self.piece + 2 * self.slots + STAT_ROWS


def project_kernel(z, gain_hbm, xp_hbm, xs_hbm, wq_hbm, wk_hbm, wv_hbm, even_ref, odd_ref, gain_ref, xp_ref, xs_ref, wq_ref, wk_ref, wv_ref, scaled_ref, query_ref, kvp_ref, kvd_ref, sems):
    me = lax.axis_index("ctx")
    depth = z.width // 2
    loads = [
        pltpu.make_async_copy(xp_hbm, xp_ref, sems.at[0]),
        pltpu.make_async_copy(xs_hbm, xs_ref, sems.at[1]),
        pltpu.make_async_copy(wk_hbm, wk_ref, sems.at[2]),
        pltpu.make_async_copy(wv_hbm, wv_ref, sems.at[3]),
    ]
    loads += [
        pltpu.make_async_copy(wq_hbm.at[pl.ds(k * depth, depth), :], wq_ref.at[k], sems.at[4 + k])
        for k in range(2)
    ]
    loads.append(pltpu.make_async_copy(gain_hbm, gain_ref, sems.at[6]))
    loads[6].start()
    for load in loads[:6]:
        load.start()
    loads[6].wait()
    gain = gain_ref[...].astype(F32)
    gain = jnp.concatenate([gain[k : k + 1, :] for k in range(gain.shape[0])], axis=1)
    squares = []
    for k, (ref, base, size) in enumerate(
        (
            (xp_ref, 0, z.prompt),
            (xs_ref, z.prompt, z.steps * z.row_total),
        )
    ):
        loads[k].wait()
        wide = ref[...].astype(F32)
        squares.append(jnp.sum(wide * wide, axis=1, keepdims=True))
        scaled_ref[base : base + size, :] = (wide * gain).astype(BF16)
    square_rows = column_to_rows(jnp.concatenate(squares, axis=0))
    pad = jnp.zeros((STAT_ROWS - z.square_lines, 128), F32)
    stats_plain = jnp.concatenate([square_rows, pad], axis=0)
    stats_split = stack_stats([square_rows])
    decode = z.steps * z.row_total
    count = z.n * z.decode_slots
    place = lax.broadcasted_iota(jnp.int32, (count, decode), 0)
    source = lax.broadcasted_iota(jnp.int32, (count, decode), 1)
    slot = place % z.decode_slots
    wanted = (
        (slot // z.rows_own) * z.row_total
        + (place // z.decode_slots) * z.rows_own
        + slot % z.rows_own
    )
    pick = ((wanted == source) & (slot < z.decode_own)).astype(F32).astype(BF16)
    ordered = jnp.dot(
        pick, scaled_ref[z.prompt : z.rows, :], preferred_element_type=F32
    ).astype(BF16)
    for c, ref in enumerate((wk_ref, wv_ref)):
        loads[2 + c].wait()
        kvp_ref[:, c * HD : (c + 1) * HD] = jnp.dot(
            scaled_ref[0 : z.prompt, :], ref[...], preferred_element_type=F32
        )
        kvd_ref[:, c * HD : (c + 1) * HD] = jnp.dot(ordered, ref[...], preferred_element_type=F32)
    loads[4].wait()
    product = jnp.dot(scaled_ref[:, :depth], wq_ref[0], preferred_element_type=F32)
    loads[5].wait()
    query_ref[...] = product + jnp.dot(
        scaled_ref[:, depth:], wq_ref[1], preferred_element_type=F32
    )
    for d in range(z.n):
        owner = jnp.bitwise_xor(me, d)
        half = owner // z.heads
        part = query_ref[
            pl.ds(pl.multiple_of(half * z.piece, 8), z.piece),
            pl.ds(pl.multiple_of(owner % z.heads * HD, HD), HD),
        ]
        kvp = kvp_ref[pl.ds(pl.multiple_of(owner * z.prompt_own, 8), z.prompt_own), :]
        kvd = kvd_ref[pl.ds(pl.multiple_of(owner * z.decode_slots, 8), z.decode_slots), :]
        ref = odd_ref if d % 2 else even_ref
        stats = stats_split if d % 2 else stats_plain
        everything = jnp.concatenate(
            [part, kvp[:, :HD], kvd[:, :HD], kvp[:, HD:], kvd[:, HD:], stats], axis=0
        )
        ref[d // 2] = everything.astype(ref.dtype)


def pair_sum_kernel(z, even_ref, got_ref, own_ref, *send_refs):
    body = z.project - STAT_ROWS
    for i in range(z.n // 2):
        got = got_ref[i].astype(F32)
        total = even_ref[i, 0:body, :] + got[0:body]
        squares = (
            even_ref[i, body : body + z.square_lines, :]
            + read_stats(got[body:], z.square_lines, 1)[0]
        )
        if i == 0:
            pad = jnp.zeros((STAT_ROWS - z.square_lines, 128), F32)
            own_ref[...] = jnp.concatenate([total, squares, pad], axis=0)
        else:
            send_refs[i - 1][...] = jnp.concatenate(
                [total, stack_stats([squares])], axis=0
            ).astype(BF16)


def finish_kernel(z, features, own_ref, *refs):
    got_refs = refs[: z.n // 2 - 1]
    query_ref, key_ref, value_ref = refs[z.n // 2 - 1 :]
    me = lax.axis_index("ctx")
    body = z.project - STAT_ROWS
    total = own_ref[0:body, :]
    squares = own_ref[body : body + z.square_lines, :]
    for ref in got_refs:
        got = ref[...].astype(F32)
        total = total + got[0:body]
        squares = squares + read_stats(got[body:], z.square_lines, 1)[0]
    inverse = lax.rsqrt(squares / features + EPSILON)
    rows = lax.broadcasted_iota(jnp.int32, (z.piece, 1), 0) + (me // z.heads) * z.piece
    factor = HD ** (-0.5) * LOG2E
    query_ref[...] = (total[0 : z.piece] * (rows_to_column(inverse, rows) * factor)).astype(BF16)
    slot = lax.broadcasted_iota(jnp.int32, (z.slots, 1), 0)
    late = slot - z.prompt_slots
    index = jnp.where(
        slot < z.prompt_slots,
        me * z.prompt_own + slot,
        z.prompt
        + (late // z.rows_own) * z.row_total
        + me * z.rows_own
        + late % z.rows_own,
    )
    own = rows_to_column(inverse, index)
    key_ref[...] = (total[z.piece : z.piece + z.slots] * own).astype(BF16)
    value_ref[...] = (total[z.piece + z.slots : z.piece + 2 * z.slots] * own).astype(BF16)


def mask_kernel(z, length_ref, visible_ref, bias_ref, extra_ref):
    me = lax.axis_index("ctx")
    live = lax.broadcasted_iota(jnp.int32, bias_ref.shape, 1) < length_ref[0]
    bias_ref[...] = jnp.where(live, 0.0, MASKED)
    row = lax.broadcasted_iota(jnp.int32, (z.rows, 1), 0)
    late = row - z.prompt
    step = late // z.row_total
    place = late - step * z.row_total
    lanes = lax.broadcasted_iota(jnp.int32, (z.rows, z.row_total), 1)
    allowed = jnp.sum(
        jnp.where(lanes == place, visible_ref[...].astype(F32), 0.0), axis=1, keepdims=True
    )
    limit = jnp.where(late < 0, row + 1, allowed.astype(jnp.int32))
    slot = lax.broadcasted_iota(jnp.int32, (z.rows, z.slots), 1)
    late_slot = slot - z.prompt_slots
    from_prompt = (slot < z.prompt_own) & (me * z.prompt_own + slot < limit)
    from_decode = (
        (late_slot >= 0)
        & (late_slot < z.decode_own)
        & (late >= 0)
        & (me * z.rows_own + late_slot % z.rows_own == place)
        & (late_slot // z.rows_own <= step)
    )
    extra_ref[...] = jnp.where(from_prompt | from_decode, 0.0, MASKED)


def attention_kernel(z, pieces, stacked, chunk, *refs):
    key_ref, value_ref, bias_ref, extra_key_ref, extra_value_ref, extra_bias_ref = refs[:6]
    query_refs = refs[6 : 6 + len(pieces)]
    out_refs = refs[6 + len(pieces) :]
    me = lax.axis_index("ctx")
    over = (((1,), (1,)), ((), ()))
    for i, d in enumerate(pieces):
        query = query_refs[i][...]
        half = jnp.bitwise_xor(me, d) // z.heads
        extra_bias = extra_bias_ref[pl.ds(pl.multiple_of(half * z.piece, 8), z.piece), :]
        found = []
        blocks = [
            (key_ref, value_ref, start, chunk) for start in range(0, key_ref.shape[0], chunk)
        ]
        blocks.append((extra_key_ref, extra_value_ref, 0, z.slots))
        for keys, values, start, size in blocks:
            score = lax.dot_general(
                query, keys[start : start + size, :], over, preferred_element_type=F32
            )
            if keys is key_ref:
                score = score + bias_ref[:, start : start + size]
            else:
                score = score + extra_bias
            top = jnp.max(score, axis=1, keepdims=True)
            weight = jnp.exp2(score - top).astype(BF16)
            beside = jnp.concatenate(
                [values[start : start + size, :], jnp.ones((size, HD), BF16)], axis=1
            )
            found.append((top, jnp.dot(weight, beside, preferred_element_type=F32)))
        highest = functools.reduce(jnp.maximum, [top for top, _ in found])
        mixed = 0.0
        for top, block in found:
            mixed = mixed + block * jnp.exp2(top - highest)
        stats = stack_stats([column_to_rows(highest), column_to_rows(mixed[:, HD : HD + 1])])
        message = jnp.concatenate([mixed[:, :HD], stats], axis=0).astype(BF16)
        if stacked:
            out_refs[0][i] = message
        else:
            out_refs[i][...] = message


def merge(z, messages):
    blocks = []
    for message in messages:
        wide = message.astype(F32)
        top, total = read_stats(wide[z.piece :], z.stat_lines, 2)
        blocks.append((top, total, wide[0 : z.piece]))
    highest = functools.reduce(jnp.maximum, [top for top, _, _ in blocks])
    index = lax.broadcasted_iota(jnp.int32, (z.piece, 1), 0)
    total = 0.0
    mixed = 0.0
    for top, block_total, block_mixed in blocks:
        scale = jnp.exp2(top - highest)
        total = total + block_total * scale
        mixed = mixed + block_mixed * rows_to_column(scale, index)
    return highest, total, mixed


def pair_merge_kernel(z, mine_sets, got_sets, *refs):
    count = len(mine_sets) + len(got_sets)
    places = [
        [ref.at[k] for ref, size in zip(block, sizes) for k in range(size)]
        for block, sizes in ((refs, mine_sets), (refs[len(mine_sets) :], got_sets))
    ]
    for send_ref, mine_ref, got_ref in zip(refs[count:], *places):
        highest, total, mixed = merge(z, [mine_ref[...], got_ref[...]])
        send_ref[...] = jnp.concatenate([mixed, stack_stats([highest, total])], axis=0).astype(BF16)


def final_merge_kernel(z, *refs):
    out_ref = refs[-1]
    _, total, mixed = merge(z, [ref[...] for ref in refs[:-1]])
    index = lax.broadcasted_iota(jnp.int32, (z.piece, 1), 0)
    out_ref[...] = (mixed / rows_to_column(total, index)).astype(BF16)


def share_order(groups):
    return list(range(2, groups)) + [1, 0]


def output_kernel(z, weight_ref, *refs):
    piece_refs = refs[: z.n]
    *out_refs, sum_ref = refs[z.n :]
    me = lax.axis_index("ctx")
    if z.halves > 1:
        sum_ref[...] = jnp.zeros_like(sum_ref)
    total = None
    swapped = me % 2 == 1
    for d in range(0, z.n, 2):
        owner = jnp.bitwise_xor(me, d)
        first, second = piece_refs[d][...], piece_refs[d + 1][...]
        both = jnp.where(
            swapped,
            jnp.concatenate([second, first], axis=1),
            jnp.concatenate([first, second], axis=1),
        )
        product = jnp.dot(
            both,
            weight_ref[pl.ds(pl.multiple_of(owner % z.heads // 2 * 2 * HD, 2 * HD), 2 * HD), :],
            preferred_element_type=F32,
        )
        if z.halves == 1:
            total = product if total is None else total + product
        else:
            where = pl.ds(pl.multiple_of((owner // z.heads) * z.piece, 8), z.piece)
            sum_ref[where, :] = sum_ref[where, :] + product
    if z.halves == 1:
        sum_ref[...] = total
    place = lax.axis_index("kv")
    columns = sum_ref.shape[1]
    prompt_share = z.prompt // z.groups
    step_share = z.row_total // z.groups
    for out_ref, e in zip(out_refs, share_order(z.groups)):
        target = jnp.bitwise_xor(place, e)
        rows = [sum_ref[pl.ds(pl.multiple_of(target * prompt_share, 8), prompt_share), :]]
        for s in range(z.steps):
            start = z.prompt + s * z.row_total + target * step_share
            rows.append(sum_ref[pl.ds(pl.multiple_of(start, 8), step_share), :])
        share = jnp.concatenate(rows, axis=0)
        out_ref[...] = jnp.concatenate(
            [share[:, : columns // 2], share[:, columns // 2 :]], axis=0
        ).astype(BF16)


def share_sum_kernel(z, *refs):
    prompt_ref, step_ref = refs[z.groups :]
    total = refs[0][...].astype(F32)
    for ref in refs[1 : z.groups]:
        total = total + ref[...].astype(F32)
    prompt_share = z.prompt // z.groups
    step_share = z.row_total // z.groups
    half = total.shape[0] // 2
    columns = total.shape[1]
    for c in range(2):
        rows = total[c * half : (c + 1) * half]
        where = slice(c * columns, (c + 1) * columns)
        prompt_ref[:, where] = rows[0:prompt_share].astype(BF16)
        for s in range(z.steps):
            start = prompt_share + s * step_share
            step_ref[s, :, where] = rows[start : start + step_share].astype(BF16)


def swap(x, axis, size, d):
    return lax.ppermute(x, axis, [(i, i ^ d) for i in range(size)])


def on_device(
    prompt_in,
    step_in,
    norm_gain,
    query_weight,
    key_weight,
    value_weight,
    out_weight,
    key_cache,
    value_cache,
    cache_lengths,
    visible,
):
    n = lax.axis_size("ctx")
    groups = lax.axis_size("kv")
    z = Sizes(prompt_in, step_in, query_weight, visible, n, groups)
    pairs = n // 2

    cache_slots = key_cache.shape[1]
    def masks(lengths, seen):
        return call(
            functools.partial(mask_kernel, z),
            [shape(1, cache_slots, F32), shape(z.rows, z.slots, F32)],
            (lengths, seen.reshape(1, z.row_total)),
            "masks",
            1e6,
            smem=1,
        )

    even, odd = call(
        functools.partial(project_kernel, z),
        [shape(z.project, HD, F32, pairs), shape(z.project, HD, BF16, pairs)],
        (
            norm_gain.reshape(z.width // 128, 128),
            prompt_in,
            step_in.reshape(z.steps * z.row_total, z.width),
            query_weight,
            key_weight,
            value_weight,
        ),
        "project",
        2 * z.rows * z.width * (z.heads + 2) * HD,
        far=6,
        scratch=[
            pltpu.VMEM((z.width // 128, 128), BF16),
            pltpu.VMEM((z.prompt, z.width), BF16),
            pltpu.VMEM((z.steps * z.row_total, z.width), BF16),
            pltpu.VMEM((2, z.width // 2, z.heads * HD), BF16),
            pltpu.VMEM((z.width, HD), BF16),
            pltpu.VMEM((z.width, HD), BF16),
            pltpu.VMEM((z.rows, z.width), BF16),
            pltpu.VMEM((z.rows, z.heads * HD), F32),
            pltpu.VMEM((z.prompt, 2 * HD), F32),
            pltpu.VMEM((z.n * z.decode_slots, 2 * HD), F32),
            pltpu.SemaphoreType.DMA((7,)),
        ],
    )
    got = swap(odd, "ctx", n, 1)
    own, *sends = call(
        functools.partial(pair_sum_kernel, z),
        [shape(z.project, HD, F32)] + [shape(z.project, HD, BF16)] * (pairs - 1),
        (even, got),
        "pair_sum",
        1e6,
    )
    visible, *sends = lax.optimization_barrier((visible, *sends))
    gots = [swap(send, "ctx", n, 2 * (i + 1)) for i, send in enumerate(sends)]
    bias, extra_bias = masks(cache_lengths, visible)
    own, bias, extra_bias = lax.optimization_barrier((own, bias, extra_bias))
    query, extra_key, extra_value = call(
        functools.partial(finish_kernel, z, z.width * n),
        [shape(z.piece, HD, BF16), shape(z.slots, HD, BF16), shape(z.slots, HD, BF16)],
        (own, *gots),
        "finish",
        1e6,
    )

    queries = {1: swap(query, "ctx", n, 1)}
    for i in range(1, pairs):
        queries[2 * i] = swap(query, "ctx", n, 2 * i)

    def attend(pieces, stacked, name):
        message = shape(z.message, HD, BF16)
        outs = [shape(z.message, HD, BF16, len(pieces))] if stacked else [message] * len(pieces)
        chunk = 1024 if cache_slots % 1024 == 0 else cache_slots
        return call(
            functools.partial(attention_kernel, z, pieces, stacked, chunk),
            outs,
            (key_cache[0], value_cache[0], bias, extra_key, extra_value, extra_bias)
            + tuple(queries[d] for d in pieces),
            name,
            8 * len(pieces) * z.piece * cache_slots * HD,
            )

    (first_odd,) = attend((1,), False, "attend_core")
    first_odd, *passed = lax.optimization_barrier(
        (first_odd, *[queries[2 * i] for i in range(1, pairs)])
    )
    for i in range(1, pairs):
        queries[2 * i] = passed[i - 1]
        queries[2 * i + 1] = swap(queries[2 * i], "ctx", n, 1)
    odd = [tuple(range(3, n, 2)[k : k + AT_ONCE]) for k in range(0, pairs - 1, AT_ONCE)]
    even = [(2,)] + [
        tuple(range(4, n, 2)[k : k + AT_ONCE]) for k in range(0, pairs - 2, AT_ONCE)
    ]
    early = attend(even[0], True, "attend_near")
    early, *passed = lax.optimization_barrier((early, *[queries[d] for d in range(3, n, 2)]))
    queries.update(zip(range(3, n, 2), passed))
    rest_odd = [attend(pieces, True, f"attend_odd{k}")[0] for k, pieces in enumerate(odd)]
    got_first = swap(first_odd, "ctx", n, 1)
    got_rest = [swap(block, "ctx", n, 1) for block in rest_odd]
    rest = list(early) + [
        attend(pieces, True, f"attend_even{k}")[0] for k, pieces in enumerate(even[1:])
    ]

    message = shape(z.message, HD, BF16)
    sends = call(
        functools.partial(
            pair_merge_kernel, z, [len(x) for x in even], [len(x) for x in odd]
        ),
        [message] * (pairs - 1),
        (*rest, *got_rest),
        "pair_merge",
        1e6,
    )
    query, *sends = lax.optimization_barrier((query, *sends))
    gots = [swap(send, "ctx", n, 2 * (i + 1)) for i, send in enumerate(sends)]
    queries[0] = query
    (own,) = attend((0,), False, "attend_own")
    (attended,) = call(
        functools.partial(final_merge_kernel, z),
        [shape(z.piece, HD, BF16)],
        (own, got_first, *gots),
        "final_merge",
        1e6,
    )
    heads = {0: attended}
    for i in range(1, pairs):
        heads[2 * i] = swap(attended, "ctx", n, 2 * i)
    heads[1] = swap(attended, "ctx", n, 1)
    for i in range(1, pairs):
        heads[2 * i + 1] = swap(heads[2 * i], "ctx", n, 1)

    columns = out_weight.shape[1]
    share_rows = 2 * z.rows // groups
    share = shape(share_rows, columns // 2, BF16)
    shares = call(
        functools.partial(output_kernel, z),
        [share] * groups,
        (out_weight,) + tuple(heads[d] for d in range(n)),
        "output",
        2 * z.rows * z.heads * HD * columns,
        scratch=[pltpu.VMEM((z.rows, columns), F32)],
    )
    shares = [
        swap(x, "kv", groups, e) if e else x for x, e in zip(shares, share_order(groups))
    ]
    prompt_out, step_out = call(
        functools.partial(share_sum_kernel, z),
        [
            shape(z.prompt // groups, columns, BF16),
            shape(z.row_total // groups, columns, BF16, z.steps),
        ],
        tuple(shares),
        "share_sum",
        1e6,
    )
    return (prompt_out, step_out)


def solution(mesh):
    placed = (
        P(None, "ctx"),
        P(None, None, "ctx"),
        P("ctx"),
        P("ctx", "kv"),
        P("ctx", "kv"),
        P("ctx", "kv"),
        P("kv", "ctx"),
        P("kv", "ctx", None),
        P("kv", "ctx", None),
        P("ctx"),
        P(),
    )
    return jax.shard_map(
        on_device,
        mesh=mesh,
        in_specs=placed,
        out_specs=(P("kv", "ctx"), P(None, "kv", "ctx")),
        check_vma=False,
    )
```

```python
import functools

import jax
import jax.numpy as jnp
from jax import lax
from jax.experimental import pallas as pl
from jax.experimental.pallas import tpu as pltpu
from jax.sharding import PartitionSpec as P

HD = 128
EPSILON = 1e-05
MASKED = -1e30
LOG2E = 1.4426950408889634
SCALE = LOG2E / HD**0.5
STAT_ROWS = 16
AT_ONCE = 3
CHUNK = 1024
FIRST = 256
BLOCK = 512
TOO_LARGE = 2.0**60
VMEM_BYTES = 20 * 2**20
BF16 = jnp.bfloat16
F32 = jnp.float32


def up(count, multiple):
    return -(-count // multiple) * multiple


def split3(x):
    high = x.astype(BF16).astype(F32)
    rest = x - high
    middle = rest.astype(BF16).astype(F32)
    return high, middle, rest - middle


def pack_sums(z, total, squares):
    query = total[0 : z.piece]
    high = query.astype(BF16).astype(F32)
    return jnp.concatenate(
        [high, query - high, total[z.piece : z.body], stack_stats([squares])], axis=0
    ).astype(BF16)


def unpack_sums(z, sent):
    wide = sent.astype(F32)
    query = wide[0 : z.piece] + wide[z.piece : 2 * z.piece]
    total = jnp.concatenate([query, wide[2 * z.piece : z.piece + z.body]], axis=0)
    return total, read_stats(wide[z.piece + z.body :], z.square_lines, 1)[0]


def column_to_rows(column):
    count = column.shape[0]
    rows = []
    for start in range(0, count, 128):
        size = min(128, count - start)
        part = jnp.broadcast_to(column[start : start + size], (size, 128))
        on = lax.broadcasted_iota(jnp.int32, (size, 128), 0) == lax.broadcasted_iota(
            jnp.int32, (size, 128), 1
        )
        rows.append(jnp.sum(jnp.where(on, part, 0.0), axis=0, keepdims=True))
    return jnp.concatenate(rows, axis=0)


def rows_to_column(rows, index):
    total = 0.0
    for k in range(rows.shape[0]):
        lanes = lax.broadcasted_iota(jnp.int32, (index.shape[0], 128), 1) + 128 * k
        total = total + jnp.sum(
            jnp.where(lanes == index, rows[k : k + 1, :], 0.0), axis=1, keepdims=True
        )
    return total


def stack_stats(rows_list):
    parts = []
    for rows in rows_list:
        parts.extend(split3(rows))
    used = sum(part.shape[0] for part in parts)
    parts.append(jnp.zeros((STAT_ROWS - used, 128), F32))
    return jnp.concatenate(parts, axis=0)


def read_stats(block, count, kinds):
    out = []
    for kind in range(kinds):
        base = kind * 3 * count
        out.append(
            block[base : base + count]
            + block[base + count : base + 2 * count]
            + block[base + 2 * count : base + 3 * count]
        )
    return out


def call(kernel, out_shape, args, name, flops, smem=0, far=0, grant=VMEM_BYTES, scratch=()):
    whole = pl.BlockSpec(memory_space=pltpu.VMEM)
    scalar = pl.BlockSpec(memory_space=pltpu.SMEM)
    near = len(args) - far
    args = args[:near] + tuple(
        pltpu.with_memory_space_constraint(x, pltpu.HBM) for x in args[near:]
    )
    return pl.pallas_call(
        kernel,
        out_shape=out_shape,
        in_specs=[scalar] * smem
        + [whole] * (near - smem)
        + [pl.BlockSpec(memory_space=pltpu.HBM)] * far,
        out_specs=jax.tree.map(lambda _: whole, out_shape),
        scratch_shapes=list(scratch),
        compiler_params=pltpu.CompilerParams(vmem_limit_bytes=grant),
        cost_estimate=pl.CostEstimate(
            flops=int(flops), bytes_accessed=1 << 20, transcendentals=0
        ),
        name=name,
    )(*args)


def shape(rows, columns, dtype, *lead):
    return jax.ShapeDtypeStruct(tuple(lead) + (rows, columns), dtype)


class Sizes:
    def __init__(self, prompt_in, step_in, query_weight, visible, devices, groups):
        self.n = devices
        self.groups = groups
        self.prompt = prompt_in.shape[0]
        self.steps = step_in.shape[0]
        self.row_total = visible.shape[0]
        self.rows = self.prompt + self.steps * self.row_total
        self.width = prompt_in.shape[1]
        self.heads = query_weight.shape[1] // HD
        self.halves = devices // self.heads
        self.piece = self.rows // self.halves
        self.stat_lines = up(self.piece, 128) // 128
        self.square_lines = up(self.rows, 128) // 128
        self.prompt_own = self.prompt // devices
        self.rows_own = self.row_total // devices
        self.decode_own = self.rows_own * self.steps
        self.decode_slots = up(self.decode_own, 16)
        self.prompt_slots = up(self.prompt_own, 16)
        self.slots = self.prompt_slots + self.decode_slots
        self.message = self.piece + STAT_ROWS
        self.body = self.piece + 2 * self.slots
        self.project = self.body + STAT_ROWS
        self.sent = self.piece + self.project


def project_kernel(z, gain_hbm, xp_hbm, xs_hbm, wq_hbm, wk_hbm, wv_hbm, even_ref, odd_ref, gain_ref, xp_ref, xs_ref, wq_ref, wk_ref, wv_ref, scaled_ref, query_ref, kvp_ref, kvd_ref, sems):
    me = lax.axis_index("ctx")
    depth = z.width // 2
    loads = [
        pltpu.make_async_copy(xp_hbm, xp_ref, sems.at[0]),
        pltpu.make_async_copy(xs_hbm, xs_ref, sems.at[1]),
        pltpu.make_async_copy(wk_hbm, wk_ref, sems.at[2]),
        pltpu.make_async_copy(wv_hbm, wv_ref, sems.at[3]),
    ]
    loads += [
        pltpu.make_async_copy(wq_hbm.at[pl.ds(k * depth, depth), :], wq_ref.at[k], sems.at[4 + k])
        for k in range(2)
    ]
    loads.append(pltpu.make_async_copy(gain_hbm, gain_ref, sems.at[6]))
    loads[6].start()
    for load in loads[:6]:
        load.start()
    loads[6].wait()
    gain = gain_ref[...].astype(F32)
    gain = jnp.concatenate([gain[k : k + 1, :] for k in range(gain.shape[0])], axis=1)
    squares = []
    for k, (ref, base, size) in enumerate(
        (
            (xp_ref, 0, z.prompt),
            (xs_ref, z.prompt, z.steps * z.row_total),
        )
    ):
        loads[k].wait()
        wide = ref[...].astype(F32)
        squares.append(jnp.sum(wide * wide, axis=1, keepdims=True))
        scaled_ref[base : base + size, :] = (wide * gain).astype(BF16)
    square_rows = column_to_rows(jnp.concatenate(squares, axis=0))
    pad = jnp.zeros((STAT_ROWS - z.square_lines, 128), F32)
    decode = z.steps * z.row_total
    count = z.n * z.decode_slots
    place = lax.broadcasted_iota(jnp.int32, (count, decode), 0)
    source = lax.broadcasted_iota(jnp.int32, (count, decode), 1)
    slot = place % z.decode_slots
    wanted = (
        (slot // z.rows_own) * z.row_total
        + (place // z.decode_slots) * z.rows_own
        + slot % z.rows_own
    )
    pick = ((wanted == source) & (slot < z.decode_own)).astype(F32).astype(BF16)
    ordered = jnp.dot(
        pick, scaled_ref[z.prompt : z.rows, :], preferred_element_type=F32
    ).astype(BF16)
    for c, ref in enumerate((wk_ref, wv_ref)):
        loads[2 + c].wait()
        kvp_ref[:, c * HD : (c + 1) * HD] = jnp.dot(
            scaled_ref[0 : z.prompt, :], ref[...], preferred_element_type=F32
        )
        kvd_ref[:, c * HD : (c + 1) * HD] = jnp.dot(ordered, ref[...], preferred_element_type=F32)
    loads[4].wait()
    product = jnp.dot(scaled_ref[:, :depth], wq_ref[0], preferred_element_type=F32)
    loads[5].wait()
    query_ref[...] = product + jnp.dot(
        scaled_ref[:, depth:], wq_ref[1], preferred_element_type=F32
    )
    for d in range(z.n):
        owner = jnp.bitwise_xor(me, d)
        half = owner // z.heads
        part = query_ref[
            pl.ds(pl.multiple_of(half * z.piece, 8), z.piece),
            pl.ds(pl.multiple_of(owner % z.heads * HD, HD), HD),
        ]
        kvp = kvp_ref[pl.ds(pl.multiple_of(owner * z.prompt_own, 8), z.prompt_own), :]
        kvd = kvd_ref[pl.ds(pl.multiple_of(owner * z.decode_slots, 8), z.decode_slots), :]
        total = jnp.concatenate([part, kvp[:, :HD], kvd[:, :HD], kvp[:, HD:], kvd[:, HD:]], axis=0)
        if d % 2:
            odd_ref[d // 2] = pack_sums(z, total, square_rows)
        else:
            even_ref[d // 2] = jnp.concatenate([total, square_rows, pad], axis=0)


def pair_sum_kernel(z, even_ref, got_ref, own_ref, *send_refs):
    for i in range(z.n // 2):
        total, squares = unpack_sums(z, got_ref[i])
        total = total + even_ref[i, 0 : z.body, :]
        squares = squares + even_ref[i, z.body : z.body + z.square_lines, :]
        if i == 0:
            pad = jnp.zeros((STAT_ROWS - z.square_lines, 128), F32)
            own_ref[...] = jnp.concatenate([total, squares, pad], axis=0)
        else:
            send_refs[i - 1][...] = pack_sums(z, total, squares)


def finish_kernel(z, features, own_ref, *refs):
    got_refs = refs[: z.n // 2 - 1]
    query_ref, key_ref, value_ref = refs[z.n // 2 - 1 :]
    me = lax.axis_index("ctx")
    total = own_ref[0 : z.body, :]
    squares = own_ref[z.body : z.body + z.square_lines, :]
    for ref in got_refs:
        got, got_squares = unpack_sums(z, ref[...])
        total = total + got
        squares = squares + got_squares
    inverse = lax.rsqrt(squares / features + EPSILON)
    rows = lax.broadcasted_iota(jnp.int32, (z.piece, 1), 0) + (me // z.heads) * z.piece
    query_ref[...] = (total[0 : z.piece] * rows_to_column(inverse, rows)).astype(BF16)
    slot = lax.broadcasted_iota(jnp.int32, (z.slots, 1), 0)
    late = slot - z.prompt_slots
    index = jnp.where(
        slot < z.prompt_slots,
        me * z.prompt_own + slot,
        z.prompt
        + (late // z.rows_own) * z.row_total
        + me * z.rows_own
        + late % z.rows_own,
    )
    own = rows_to_column(inverse, index)
    key_ref[...] = (total[z.piece : z.piece + z.slots] * own).astype(BF16)
    value_ref[...] = (total[z.piece + z.slots : z.piece + 2 * z.slots] * own).astype(BF16)


def prepare_kernel(z, length_ref, visible_ref, key_hbm, value_hbm, key_ref, value_ref, live_ref, extra_ref, sems):
    loads = [
        pltpu.make_async_copy(key_hbm, key_ref, sems.at[0]),
        pltpu.make_async_copy(value_hbm, value_ref, sems.at[1]),
    ]
    for load in loads:
        load.start()
    me = lax.axis_index("ctx")
    length = length_ref[0]
    size = min(BLOCK, key_ref.shape[0])
    blocks = key_ref.shape[0] // size
    local = lax.broadcasted_iota(jnp.int32, (size, HD), 0)

    def mark(i, carry):
        rows = pl.ds(pl.multiple_of(i * size, size), size)
        live_ref[rows, :] = jnp.where(local + i * size < length, 1.0, 0.0).astype(BF16)
        return carry

    lax.fori_loop(0, blocks, mark, 0)
    row = lax.broadcasted_iota(jnp.int32, (z.rows, 1), 0)
    late = row - z.prompt
    step = late // z.row_total
    place = late - step * z.row_total
    lanes = lax.broadcasted_iota(jnp.int32, (z.rows, z.row_total), 1)
    allowed = jnp.sum(
        jnp.where(lanes == place, visible_ref[...].astype(F32), 0.0), axis=1, keepdims=True
    )
    limit = jnp.where(late < 0, row + 1, allowed.astype(jnp.int32))
    slot = lax.broadcasted_iota(jnp.int32, (z.rows, z.slots), 1)
    late_slot = slot - z.prompt_slots
    from_prompt = (slot < z.prompt_own) & (me * z.prompt_own + slot < limit)
    from_decode = (
        (late_slot >= 0)
        & (late_slot < z.decode_own)
        & (late >= 0)
        & (me * z.rows_own + late_slot % z.rows_own == place)
        & (late_slot // z.rows_own <= step)
    )
    extra_ref[...] = jnp.where(from_prompt | from_decode, 0.0, MASKED)
    for load in loads:
        load.wait()
    stand_in = jnp.broadcast_to(key_ref[0:16, :].astype(F32)[0:1, :], (size, HD))

    def clear(i, carry):
        rows = pl.ds(pl.multiple_of(i * size, size), size)
        live = local + i * size < length
        key_ref[rows, :] = jnp.where(live, key_ref[rows, :].astype(F32), stand_in).astype(BF16)
        value_ref[rows, :] = jnp.where(live, value_ref[rows, :].astype(F32), 0.0).astype(BF16)
        return carry

    lax.fori_loop(length // size, blocks, clear, 0)


def beside(values, live):
    return jnp.concatenate([values, live], axis=1)


def attention_kernel(z, pieces, stacked, *refs):
    key_ref, value_ref, live_ref, extra_key_ref, extra_value_ref, extra_bias_ref = refs[:6]
    query_refs = refs[6 : 6 + len(pieces)]
    out_refs = refs[6 + len(pieces) :]
    me = lax.axis_index("ctx")
    over = (((1,), (1,)), ((), ()))
    slots = key_ref.shape[0]

    def scores(query, rows):
        return lax.dot_general(query, key_ref[rows, :], over, preferred_element_type=F32)

    def mix(weight, rows):
        return jnp.dot(
            weight.astype(BF16), beside(value_ref[rows, :], live_ref[rows, :]),
            preferred_element_type=F32,
        )

    def extras(query, d):
        half = jnp.bitwise_xor(me, d) // z.heads
        bias = extra_bias_ref[pl.ds(pl.multiple_of(half * z.piece, 8), z.piece), :]
        score = lax.dot_general(query, extra_key_ref[...], over, preferred_element_type=F32)
        return score + bias

    def mix_extras(weight):
        ones = jnp.ones((z.slots, HD), BF16)
        return jnp.dot(
            weight.astype(BF16), beside(extra_value_ref[...], ones), preferred_element_type=F32
        )

    def write(i, level, mixed):
        stats = stack_stats([column_to_rows(level * SCALE), column_to_rows(mixed[:, HD : HD + 1])])
        message = jnp.concatenate([mixed[:, :HD], stats], axis=0).astype(BF16)
        if stacked:
            out_refs[0][i] = message
        else:
            out_refs[i][...] = message

    first = min(FIRST, slots)
    chunk = min(CHUNK, slots)
    bounds = [0, first] + [k for k in range(chunk, slots + 1, chunk) if k > first]
    worst = None
    for i, d in enumerate(pieces):
        query = query_refs[i][...]
        score = scores(query, slice(0, first))
        level = jnp.max(score, axis=1, keepdims=True)
        mixed = mix(jnp.exp2((score - level) * SCALE), slice(0, first))
        for start, end in zip(bounds[1:], bounds[2:]):
            rows = slice(start, end)
            mixed = mixed + mix(jnp.exp2((scores(query, rows) - level) * SCALE), rows)
        mixed = mixed + mix_extras(jnp.exp2((extras(query, d) - level) * SCALE))
        write(i, level, mixed)
        over_limit = jnp.where(mixed[:, HD:] < TOO_LARGE, 0.0, 1.0)
        worst = over_limit if worst is None else jnp.maximum(worst, over_limit)

    @pl.when(jnp.max(worst) > 0.0)
    def _():
        for i, d in enumerate(pieces):
            query = query_refs[i][...]
            score = extras(query, d)
            level = jnp.max(score, axis=1, keepdims=True)
            mixed = mix_extras(jnp.exp2((score - level) * SCALE))

            def step(k, carry):
                level, mixed = carry
                rows = pl.ds(pl.multiple_of(k * chunk, chunk), chunk)
                score = scores(query, rows)
                higher = jnp.maximum(level, jnp.max(score, axis=1, keepdims=True))
                return higher, mixed * jnp.exp2((level - higher) * SCALE) + mix(
                    jnp.exp2((score - higher) * SCALE), rows
                )

            level, mixed = lax.fori_loop(0, slots // chunk, step, (level, mixed))
            write(i, level, mixed)


def merge(z, messages):
    blocks = []
    for message in messages:
        wide = message.astype(F32)
        top, total = read_stats(wide[z.piece :], z.stat_lines, 2)
        blocks.append((top, total, wide[0 : z.piece]))
    highest = functools.reduce(jnp.maximum, [top for top, _, _ in blocks])
    index = lax.broadcasted_iota(jnp.int32, (z.piece, 1), 0)
    total = 0.0
    mixed = 0.0
    for top, block_total, block_mixed in blocks:
        scale = jnp.exp2(top - highest)
        total = total + block_total * scale
        mixed = mixed + block_mixed * rows_to_column(scale, index)
    return highest, total, mixed


def pair_merge_kernel(z, mine_sets, got_sets, *refs):
    count = len(mine_sets) + len(got_sets)
    places = [
        [ref.at[k] for ref, size in zip(block, sizes) for k in range(size)]
        for block, sizes in ((refs, mine_sets), (refs[len(mine_sets) :], got_sets))
    ]
    for send_ref, mine_ref, got_ref in zip(refs[count:], *places):
        highest, total, mixed = merge(z, [mine_ref[...], got_ref[...]])
        send_ref[...] = jnp.concatenate([mixed, stack_stats([highest, total])], axis=0).astype(BF16)


def final_merge_kernel(z, *refs):
    out_ref = refs[-1]
    _, total, mixed = merge(z, [ref[...] for ref in refs[:-1]])
    index = lax.broadcasted_iota(jnp.int32, (z.piece, 1), 0)
    out_ref[...] = (mixed / rows_to_column(total, index)).astype(BF16)


def share_order(groups):
    return list(range(groups - 1, -1, -1))


def output_kernel(z, weight_ref, *refs):
    piece_refs = refs[: z.n]
    *out_refs, sum_ref = refs[z.n :]
    me = lax.axis_index("ctx")
    if z.halves > 1:
        sum_ref[...] = jnp.zeros_like(sum_ref)
    total = None
    swapped = me % 2 == 1
    for d in range(0, z.n, 2):
        owner = jnp.bitwise_xor(me, d)
        first, second = piece_refs[d][...], piece_refs[d + 1][...]
        both = jnp.where(
            swapped,
            jnp.concatenate([second, first], axis=1),
            jnp.concatenate([first, second], axis=1),
        )
        product = jnp.dot(
            both,
            weight_ref[pl.ds(pl.multiple_of(owner % z.heads // 2 * 2 * HD, 2 * HD), 2 * HD), :],
            preferred_element_type=F32,
        )
        if z.halves == 1:
            total = product if total is None else total + product
        else:
            where = pl.ds(pl.multiple_of((owner // z.heads) * z.piece, 8), z.piece)
            sum_ref[where, :] = sum_ref[where, :] + product
    if z.halves == 1:
        sum_ref[...] = total
    place = lax.axis_index("kv")
    columns = sum_ref.shape[1]
    prompt_share = z.prompt // z.groups
    step_share = z.row_total // z.groups
    for out_ref, e in zip(out_refs, share_order(z.groups)):
        target = jnp.bitwise_xor(place, e)
        rows = [sum_ref[pl.ds(pl.multiple_of(target * prompt_share, 8), prompt_share), :]]
        for s in range(z.steps):
            start = z.prompt + s * z.row_total + target * step_share
            rows.append(sum_ref[pl.ds(pl.multiple_of(start, 8), step_share), :])
        share = jnp.concatenate(rows, axis=0)
        out_ref[...] = jnp.concatenate(
            [share[:, : columns // 2], share[:, columns // 2 :]], axis=0
        ).astype(BF16)


def share_sum_kernel(z, *refs):
    prompt_ref, step_ref = refs[z.groups :]
    total = refs[0][...].astype(F32)
    for ref in refs[1 : z.groups]:
        total = total + ref[...].astype(F32)
    prompt_share = z.prompt // z.groups
    step_share = z.row_total // z.groups
    half = total.shape[0] // 2
    columns = total.shape[1]
    for c in range(2):
        rows = total[c * half : (c + 1) * half]
        where = slice(c * columns, (c + 1) * columns)
        prompt_ref[:, where] = rows[0:prompt_share].astype(BF16)
        for s in range(z.steps):
            start = prompt_share + s * step_share
            step_ref[s, :, where] = rows[start : start + step_share].astype(BF16)


def swap(x, axis, size, d):
    return lax.ppermute(x, axis, [(i, i ^ d) for i in range(size)])


def on_device(
    prompt_in,
    step_in,
    norm_gain,
    query_weight,
    key_weight,
    value_weight,
    out_weight,
    key_cache,
    value_cache,
    cache_lengths,
    visible,
):
    n = lax.axis_size("ctx")
    groups = lax.axis_size("kv")
    z = Sizes(prompt_in, step_in, query_weight, visible, n, groups)
    pairs = n // 2

    cache_slots = key_cache.shape[1]
    cache = shape(cache_slots, HD, BF16)

    def prepare(lengths, seen):
        return call(
            functools.partial(prepare_kernel, z),
            [cache, cache, cache, shape(z.rows, z.slots, F32)],
            (lengths, seen.reshape(1, z.row_total), key_cache[0], value_cache[0]),
            "prepare",
            1e6,
            smem=1,
            far=2,
            scratch=[pltpu.SemaphoreType.DMA((2,))],
        )

    even, odd = call(
        functools.partial(project_kernel, z),
        [shape(z.project, HD, F32, pairs), shape(z.sent, HD, BF16, pairs)],
        (
            norm_gain.reshape(z.width // 128, 128),
            prompt_in,
            step_in.reshape(z.steps * z.row_total, z.width),
            query_weight,
            key_weight,
            value_weight,
        ),
        "project",
        2 * z.rows * z.width * (z.heads + 2) * HD,
        far=6,
        scratch=[
            pltpu.VMEM((z.width // 128, 128), BF16),
            pltpu.VMEM((z.prompt, z.width), BF16),
            pltpu.VMEM((z.steps * z.row_total, z.width), BF16),
            pltpu.VMEM((2, z.width // 2, z.heads * HD), BF16),
            pltpu.VMEM((z.width, HD), BF16),
            pltpu.VMEM((z.width, HD), BF16),
            pltpu.VMEM((z.rows, z.width), BF16),
            pltpu.VMEM((z.rows, z.heads * HD), F32),
            pltpu.VMEM((z.prompt, 2 * HD), F32),
            pltpu.VMEM((z.n * z.decode_slots, 2 * HD), F32),
            pltpu.SemaphoreType.DMA((7,)),
        ],
    )
    got = swap(odd, "ctx", n, 1)
    own, *sends = call(
        functools.partial(pair_sum_kernel, z),
        [shape(z.project, HD, F32)] + [shape(z.sent, HD, BF16)] * (pairs - 1),
        (even, got),
        "pair_sum",
        1e6,
    )
    visible, *sends = lax.optimization_barrier((visible, *sends))
    gots = [swap(send, "ctx", n, 2 * (i + 1)) for i, send in enumerate(sends)]
    keys, values, live, extra_bias = prepare(cache_lengths, visible)
    own, keys, values, live, extra_bias = lax.optimization_barrier(
        (own, keys, values, live, extra_bias)
    )
    query, extra_key, extra_value = call(
        functools.partial(finish_kernel, z, z.width * n),
        [shape(z.piece, HD, BF16), shape(z.slots, HD, BF16), shape(z.slots, HD, BF16)],
        (own, *gots),
        "finish",
        1e6,
    )

    queries = {1: swap(query, "ctx", n, 1)}
    for i in range(1, pairs):
        queries[2 * i] = swap(query, "ctx", n, 2 * i)

    def attend(pieces, stacked, name):
        message = shape(z.message, HD, BF16)
        outs = [shape(z.message, HD, BF16, len(pieces))] if stacked else [message] * len(pieces)
        return call(
            functools.partial(attention_kernel, z, pieces, stacked),
            outs,
            (keys, values, live, extra_key, extra_value, extra_bias)
            + tuple(queries[d] for d in pieces),
            name,
            8 * len(pieces) * z.piece * cache_slots * HD,
            )

    (first_odd,) = attend((1,), False, "attend_core")
    first_odd, *passed = lax.optimization_barrier(
        (first_odd, *[queries[2 * i] for i in range(1, pairs)])
    )
    for i in range(1, pairs):
        queries[2 * i] = passed[i - 1]
        queries[2 * i + 1] = swap(queries[2 * i], "ctx", n, 1)
    odd = [tuple(range(3, n, 2)[k : k + AT_ONCE]) for k in range(0, pairs - 1, AT_ONCE)]
    even = [(2,)] + [
        tuple(range(4, n, 2)[k : k + AT_ONCE]) for k in range(0, pairs - 2, AT_ONCE)
    ]
    early = attend(even[0], True, "attend_near")
    early, *passed = lax.optimization_barrier((early, *[queries[d] for d in range(3, n, 2)]))
    queries.update(zip(range(3, n, 2), passed))
    rest_odd = [attend(pieces, True, f"attend_odd{k}")[0] for k, pieces in enumerate(odd)]
    got_first = swap(first_odd, "ctx", n, 1)
    got_rest = [swap(block, "ctx", n, 1) for block in rest_odd]
    rest = list(early) + [
        attend(pieces, True, f"attend_even{k}")[0] for k, pieces in enumerate(even[1:])
    ]

    message = shape(z.message, HD, BF16)
    sends = call(
        functools.partial(
            pair_merge_kernel, z, [len(x) for x in even], [len(x) for x in odd]
        ),
        [message] * (pairs - 1),
        (*rest, *got_rest),
        "pair_merge",
        1e6,
    )
    query, *sends = lax.optimization_barrier((query, *sends))
    gots = [swap(send, "ctx", n, 2 * (i + 1)) for i, send in enumerate(sends)]
    queries[0] = query
    (own,) = attend((0,), False, "attend_own")
    (attended,) = call(
        functools.partial(final_merge_kernel, z),
        [shape(z.piece, HD, BF16)],
        (own, got_first, *gots),
        "final_merge",
        1e6,
    )
    heads = {0: attended}
    for i in range(1, pairs):
        heads[2 * i] = swap(attended, "ctx", n, 2 * i)
    heads[1] = swap(attended, "ctx", n, 1)
    for i in range(1, pairs):
        heads[2 * i + 1] = swap(heads[2 * i], "ctx", n, 1)

    columns = out_weight.shape[1]
    share_rows = 2 * z.rows // groups
    share = shape(share_rows, columns // 2, BF16)
    shares = call(
        functools.partial(output_kernel, z),
        [share] * groups,
        (out_weight,) + tuple(heads[d] for d in range(n)),
        "output",
        2 * z.rows * z.heads * HD * columns,
        scratch=[pltpu.VMEM((z.rows, columns), F32)],
    )
    shares = [
        swap(x, "kv", groups, e) if e else x for x, e in zip(shares, share_order(groups))
    ]
    prompt_out, step_out = call(
        functools.partial(share_sum_kernel, z),
        [
            shape(z.prompt // groups, columns, BF16),
            shape(z.row_total // groups, columns, BF16, z.steps),
        ],
        tuple(shares),
        "share_sum",
        1e6,
    )
    return (prompt_out, step_out)


def solution(mesh):
    placed = (
        P(None, "ctx"),
        P(None, None, "ctx"),
        P("ctx"),
        P("ctx", "kv"),
        P("ctx", "kv"),
        P("ctx", "kv"),
        P("kv", "ctx"),
        P("kv", "ctx", None),
        P("kv", "ctx", None),
        P("ctx"),
        P(),
    )
    return jax.shard_map(
        on_device,
        mesh=mesh,
        in_specs=placed,
        out_specs=(P("kv", "ctx"), P(None, "kv", "ctx")),
        check_vma=False,
    )
```

```python
import functools

import jax
import jax.numpy as jnp
from jax import lax
from jax.experimental import pallas as pl
from jax.experimental.pallas import tpu as pltpu
from jax.sharding import PartitionSpec as P

HD = 128
EPSILON = 1e-05
MASKED = -1e30
LOG2E = 1.4426950408889634
SCALE = LOG2E / HD**0.5
STAT_ROWS = 16
AT_ONCE = 3
CHUNK = 1024
FIRST = 256
BLOCK = 512
TOO_LARGE = 2.0**60
VMEM_BYTES = 20 * 2**20
BF16 = jnp.bfloat16
F32 = jnp.float32


def up(count, multiple):
    return -(-count // multiple) * multiple


def split3(x):
    high = x.astype(BF16).astype(F32)
    rest = x - high
    middle = rest.astype(BF16).astype(F32)
    return high, middle, rest - middle


def pack_sums(z, total, squares):
    query = total[0 : z.piece]
    high = query.astype(BF16).astype(F32)
    return jnp.concatenate(
        [high, query - high, total[z.piece : z.body], stack_stats([squares])], axis=0
    ).astype(BF16)


def unpack_sums(z, sent):
    wide = sent.astype(F32)
    query = wide[0 : z.piece] + wide[z.piece : 2 * z.piece]
    total = jnp.concatenate([query, wide[2 * z.piece : z.piece + z.body]], axis=0)
    return total, read_stats(wide[z.piece + z.body :], z.square_lines, 1)[0]


def column_to_rows(column):
    count = column.shape[0]
    rows = []
    for start in range(0, count, 128):
        size = min(128, count - start)
        part = jnp.broadcast_to(column[start : start + size], (size, 128))
        on = lax.broadcasted_iota(jnp.int32, (size, 128), 0) == lax.broadcasted_iota(
            jnp.int32, (size, 128), 1
        )
        rows.append(jnp.sum(jnp.where(on, part, 0.0), axis=0, keepdims=True))
    return jnp.concatenate(rows, axis=0)


def rows_to_column(rows, index):
    total = 0.0
    for k in range(rows.shape[0]):
        lanes = lax.broadcasted_iota(jnp.int32, (index.shape[0], 128), 1) + 128 * k
        total = total + jnp.sum(
            jnp.where(lanes == index, rows[k : k + 1, :], 0.0), axis=1, keepdims=True
        )
    return total


def stack_stats(rows_list):
    parts = []
    for rows in rows_list:
        parts.extend(split3(rows))
    used = sum(part.shape[0] for part in parts)
    parts.append(jnp.zeros((STAT_ROWS - used, 128), F32))
    return jnp.concatenate(parts, axis=0)


def read_stats(block, count, kinds):
    out = []
    for kind in range(kinds):
        base = kind * 3 * count
        out.append(
            block[base : base + count]
            + block[base + count : base + 2 * count]
            + block[base + 2 * count : base + 3 * count]
        )
    return out


def call(kernel, out_shape, args, name, flops, smem=0, far=0, grant=VMEM_BYTES, scratch=()):
    whole = pl.BlockSpec(memory_space=pltpu.VMEM)
    scalar = pl.BlockSpec(memory_space=pltpu.SMEM)
    near = len(args) - far
    args = args[:near] + tuple(
        pltpu.with_memory_space_constraint(x, pltpu.HBM) for x in args[near:]
    )
    return pl.pallas_call(
        kernel,
        out_shape=out_shape,
        in_specs=[scalar] * smem
        + [whole] * (near - smem)
        + [pl.BlockSpec(memory_space=pltpu.HBM)] * far,
        out_specs=jax.tree.map(lambda _: whole, out_shape),
        scratch_shapes=list(scratch),
        compiler_params=pltpu.CompilerParams(vmem_limit_bytes=grant),
        cost_estimate=pl.CostEstimate(
            flops=int(flops), bytes_accessed=1 << 20, transcendentals=0
        ),
        name=name,
    )(*args)


def shape(rows, columns, dtype, *lead):
    return jax.ShapeDtypeStruct(tuple(lead) + (rows, columns), dtype)


class Sizes:
    def __init__(self, prompt_in, step_in, query_weight, visible, devices, groups):
        self.n = devices
        self.groups = groups
        self.prompt = prompt_in.shape[0]
        self.steps = step_in.shape[0]
        self.row_total = visible.shape[0]
        self.rows = self.prompt + self.steps * self.row_total
        self.width = prompt_in.shape[1]
        self.heads = query_weight.shape[1] // HD
        self.halves = devices // self.heads
        self.piece = self.rows // self.halves
        self.stat_lines = up(self.piece, 128) // 128
        self.square_lines = up(self.rows, 128) // 128
        self.prompt_own = self.prompt // devices
        self.rows_own = self.row_total // devices
        self.decode_own = self.rows_own * self.steps
        self.decode_slots = up(self.decode_own, 16)
        self.prompt_slots = up(self.prompt_own, 16)
        self.slots = self.prompt_slots + self.decode_slots
        self.message = self.piece + STAT_ROWS
        self.body = self.piece + 2 * self.slots
        self.project = self.body + STAT_ROWS
        self.sent = self.piece + self.project


def project_kernel(z, gain_hbm, xp_hbm, xs_hbm, wq_hbm, wk_hbm, wv_hbm, even_ref, odd_ref, gain_ref, xp_ref, xs_ref, wq_ref, wk_ref, wv_ref, scaled_ref, query_ref, kvp_ref, kvd_ref, sems):
    me = lax.axis_index("ctx")
    depth = z.width // 2
    loads = [
        pltpu.make_async_copy(xp_hbm, xp_ref, sems.at[0]),
        pltpu.make_async_copy(xs_hbm, xs_ref, sems.at[1]),
        pltpu.make_async_copy(wk_hbm, wk_ref, sems.at[2]),
        pltpu.make_async_copy(wv_hbm, wv_ref, sems.at[3]),
    ]
    loads += [
        pltpu.make_async_copy(wq_hbm.at[pl.ds(k * depth, depth), :], wq_ref.at[k], sems.at[4 + k])
        for k in range(2)
    ]
    loads.append(pltpu.make_async_copy(gain_hbm, gain_ref, sems.at[6]))
    loads[6].start()
    for load in loads[:6]:
        load.start()
    loads[6].wait()
    gain = gain_ref[...].astype(F32)
    gain = jnp.concatenate([gain[k : k + 1, :] for k in range(gain.shape[0])], axis=1)
    squares = []
    for k, (ref, base, size) in enumerate(
        (
            (xp_ref, 0, z.prompt),
            (xs_ref, z.prompt, z.steps * z.row_total),
        )
    ):
        loads[k].wait()
        wide = ref[...].astype(F32)
        squares.append(jnp.sum(wide * wide, axis=1, keepdims=True))
        scaled_ref[base : base + size, :] = (wide * gain).astype(BF16)
    square_rows = column_to_rows(jnp.concatenate(squares, axis=0))
    pad = jnp.zeros((STAT_ROWS - z.square_lines, 128), F32)
    decode = z.steps * z.row_total
    count = z.n * z.decode_slots
    place = lax.broadcasted_iota(jnp.int32, (count, decode), 0)
    source = lax.broadcasted_iota(jnp.int32, (count, decode), 1)
    slot = place % z.decode_slots
    wanted = (
        (slot // z.rows_own) * z.row_total
        + (place // z.decode_slots) * z.rows_own
        + slot % z.rows_own
    )
    pick = ((wanted == source) & (slot < z.decode_own)).astype(F32).astype(BF16)
    ordered = jnp.dot(
        pick, scaled_ref[z.prompt : z.rows, :], preferred_element_type=F32
    ).astype(BF16)
    for c, ref in enumerate((wk_ref, wv_ref)):
        loads[2 + c].wait()
        kvp_ref[:, c * HD : (c + 1) * HD] = jnp.dot(
            scaled_ref[0 : z.prompt, :], ref[...], preferred_element_type=F32
        )
        kvd_ref[:, c * HD : (c + 1) * HD] = jnp.dot(ordered, ref[...], preferred_element_type=F32)
    loads[4].wait()
    product = jnp.dot(scaled_ref[:, :depth], wq_ref[0], preferred_element_type=F32)
    loads[5].wait()
    query_ref[...] = product + jnp.dot(
        scaled_ref[:, depth:], wq_ref[1], preferred_element_type=F32
    )
    for d in range(z.n):
        owner = jnp.bitwise_xor(me, d)
        half = owner // z.heads
        part = query_ref[
            pl.ds(pl.multiple_of(half * z.piece, 8), z.piece),
            pl.ds(pl.multiple_of(owner % z.heads * HD, HD), HD),
        ]
        kvp = kvp_ref[pl.ds(pl.multiple_of(owner * z.prompt_own, 8), z.prompt_own), :]
        kvd = kvd_ref[pl.ds(pl.multiple_of(owner * z.decode_slots, 8), z.decode_slots), :]
        total = jnp.concatenate([part, kvp[:, :HD], kvd[:, :HD], kvp[:, HD:], kvd[:, HD:]], axis=0)
        if d % 2:
            odd_ref[d // 2] = pack_sums(z, total, square_rows)
        else:
            even_ref[d // 2] = jnp.concatenate([total, square_rows, pad], axis=0)


def pair_sum_kernel(z, even_ref, got_ref, own_ref, *send_refs):
    for i in range(z.n // 2):
        total, squares = unpack_sums(z, got_ref[i])
        total = total + even_ref[i, 0 : z.body, :]
        squares = squares + even_ref[i, z.body : z.body + z.square_lines, :]
        if i == 0:
            pad = jnp.zeros((STAT_ROWS - z.square_lines, 128), F32)
            own_ref[...] = jnp.concatenate([total, squares, pad], axis=0)
        else:
            send_refs[i - 1][...] = pack_sums(z, total, squares)


def finish_kernel(z, features, own_ref, *refs):
    got_refs = refs[: z.n // 2 - 1]
    query_ref, key_ref, value_ref = refs[z.n // 2 - 1 :]
    me = lax.axis_index("ctx")
    total = own_ref[0 : z.body, :]
    squares = own_ref[z.body : z.body + z.square_lines, :]
    for ref in got_refs:
        got, got_squares = unpack_sums(z, ref[...])
        total = total + got
        squares = squares + got_squares
    inverse = lax.rsqrt(squares / features + EPSILON)
    rows = lax.broadcasted_iota(jnp.int32, (z.piece, 1), 0) + (me // z.heads) * z.piece
    query_ref[...] = (total[0 : z.piece] * rows_to_column(inverse, rows)).astype(BF16)
    slot = lax.broadcasted_iota(jnp.int32, (z.slots, 1), 0)
    late = slot - z.prompt_slots
    index = jnp.where(
        slot < z.prompt_slots,
        me * z.prompt_own + slot,
        z.prompt
        + (late // z.rows_own) * z.row_total
        + me * z.rows_own
        + late % z.rows_own,
    )
    own = rows_to_column(inverse, index)
    key_ref[...] = (total[z.piece : z.piece + z.slots] * own).astype(BF16)
    value_ref[...] = (total[z.piece + z.slots : z.piece + 2 * z.slots] * own).astype(BF16)


def prepare_kernel(z, length_ref, visible_ref, key_hbm, value_hbm, key_ref, value_ref, live_ref, extra_ref, sems):
    loads = [
        pltpu.make_async_copy(key_hbm, key_ref, sems.at[0]),
        pltpu.make_async_copy(value_hbm, value_ref, sems.at[1]),
    ]
    for load in loads:
        load.start()
    me = lax.axis_index("ctx")
    length = length_ref[0]
    size = min(BLOCK, key_ref.shape[0])
    blocks = key_ref.shape[0] // size
    local = lax.broadcasted_iota(jnp.int32, (size, HD), 0)

    def mark(i, carry):
        rows = pl.ds(pl.multiple_of(i * size, size), size)
        live_ref[rows, :] = jnp.where(local + i * size < length, 1.0, 0.0).astype(BF16)
        return carry

    lax.fori_loop(0, blocks, mark, 0)
    row = lax.broadcasted_iota(jnp.int32, (z.rows, 1), 0)
    late = row - z.prompt
    step = late // z.row_total
    place = late - step * z.row_total
    lanes = lax.broadcasted_iota(jnp.int32, (z.rows, z.row_total), 1)
    allowed = jnp.sum(
        jnp.where(lanes == place, visible_ref[...].astype(F32), 0.0), axis=1, keepdims=True
    )
    limit = jnp.where(late < 0, row + 1, allowed.astype(jnp.int32))
    slot = lax.broadcasted_iota(jnp.int32, (z.rows, z.slots), 1)
    late_slot = slot - z.prompt_slots
    from_prompt = (slot < z.prompt_own) & (me * z.prompt_own + slot < limit)
    from_decode = (
        (late_slot >= 0)
        & (late_slot < z.decode_own)
        & (late >= 0)
        & (me * z.rows_own + late_slot % z.rows_own == place)
        & (late_slot // z.rows_own <= step)
    )
    extra_ref[...] = jnp.where(from_prompt | from_decode, 0.0, MASKED)
    for load in loads:
        load.wait()
    stand_in = jnp.broadcast_to(key_ref[0:16, :].astype(F32)[0:1, :], (size, HD))

    def clear(i, carry):
        rows = pl.ds(pl.multiple_of(i * size, size), size)
        live = local + i * size < length
        key_ref[rows, :] = jnp.where(live, key_ref[rows, :].astype(F32), stand_in).astype(BF16)
        value_ref[rows, :] = jnp.where(live, value_ref[rows, :].astype(F32), 0.0).astype(BF16)
        return carry

    lax.fori_loop(length // size, blocks, clear, 0)


def beside(values, live):
    return jnp.concatenate([values, live], axis=1)


def attention_kernel(z, pieces, stacked, offset, *refs):
    key_ref, value_ref, live_ref, extra_key_ref, extra_value_ref, extra_bias_ref = refs[:6]
    if offset is None:
        query_refs = refs[6 : 6 + len(pieces)]
        out_refs = refs[6 + len(pieces) :]
    else:
        query_refs = [refs[6].at[offset + i] for i in range(len(pieces))]
        out_refs = refs[7:]
    me = lax.axis_index("ctx")
    over = (((1,), (1,)), ((), ()))
    slots = key_ref.shape[0]

    def scores(query, rows):
        return lax.dot_general(query, key_ref[rows, :], over, preferred_element_type=F32)

    def mix(weight, rows):
        return jnp.dot(
            weight.astype(BF16), beside(value_ref[rows, :], live_ref[rows, :]),
            preferred_element_type=F32,
        )

    def extras(query, d):
        half = jnp.bitwise_xor(me, d) // z.heads
        bias = extra_bias_ref[pl.ds(pl.multiple_of(half * z.piece, 8), z.piece), :]
        score = lax.dot_general(query, extra_key_ref[...], over, preferred_element_type=F32)
        return score + bias

    def mix_extras(weight):
        ones = jnp.ones((z.slots, HD), BF16)
        return jnp.dot(
            weight.astype(BF16), beside(extra_value_ref[...], ones), preferred_element_type=F32
        )

    def write(i, level, mixed):
        stats = stack_stats([column_to_rows(level * SCALE), column_to_rows(mixed[:, HD : HD + 1])])
        message = jnp.concatenate([mixed[:, :HD], stats], axis=0).astype(BF16)
        if stacked:
            out_refs[0][i] = message
        else:
            out_refs[i][...] = message

    first = min(FIRST, slots)
    chunk = min(CHUNK, slots)
    bounds = [0, first] + [k for k in range(chunk, slots + 1, chunk) if k > first]
    worst = None
    for i, d in enumerate(pieces):
        query = query_refs[i][...]
        score = scores(query, slice(0, first))
        level = jnp.max(score, axis=1, keepdims=True)
        mixed = mix(jnp.exp2((score - level) * SCALE), slice(0, first))
        for start, end in zip(bounds[1:], bounds[2:]):
            rows = slice(start, end)
            mixed = mixed + mix(jnp.exp2((scores(query, rows) - level) * SCALE), rows)
        mixed = mixed + mix_extras(jnp.exp2((extras(query, d) - level) * SCALE))
        write(i, level, mixed)
        over_limit = jnp.where(mixed[:, HD:] < TOO_LARGE, 0.0, 1.0)
        worst = over_limit if worst is None else jnp.maximum(worst, over_limit)

    @pl.when(jnp.max(worst) > 0.0)
    def _():
        for i, d in enumerate(pieces):
            query = query_refs[i][...]
            score = extras(query, d)
            level = jnp.max(score, axis=1, keepdims=True)
            mixed = mix_extras(jnp.exp2((score - level) * SCALE))

            def step(k, carry):
                level, mixed = carry
                rows = pl.ds(pl.multiple_of(k * chunk, chunk), chunk)
                score = scores(query, rows)
                higher = jnp.maximum(level, jnp.max(score, axis=1, keepdims=True))
                return higher, mixed * jnp.exp2((level - higher) * SCALE) + mix(
                    jnp.exp2((score - higher) * SCALE), rows
                )

            level, mixed = lax.fori_loop(0, slots // chunk, step, (level, mixed))
            write(i, level, mixed)


def merge(z, messages):
    blocks = []
    for message in messages:
        wide = message.astype(F32)
        top, total = read_stats(wide[z.piece :], z.stat_lines, 2)
        blocks.append((top, total, wide[0 : z.piece]))
    highest = functools.reduce(jnp.maximum, [top for top, _, _ in blocks])
    index = lax.broadcasted_iota(jnp.int32, (z.piece, 1), 0)
    total = 0.0
    mixed = 0.0
    for top, block_total, block_mixed in blocks:
        scale = jnp.exp2(top - highest)
        total = total + block_total * scale
        mixed = mixed + block_mixed * rows_to_column(scale, index)
    return highest, total, mixed


def pair_merge_kernel(z, mine_sets, got_sets, *refs):
    count = len(mine_sets) + len(got_sets)
    places = [
        [ref.at[k] for ref, size in zip(block, sizes) for k in range(size)]
        for block, sizes in ((refs, mine_sets), (refs[len(mine_sets) :], got_sets))
    ]
    for send_ref, mine_ref, got_ref in zip(refs[count:], *places):
        highest, total, mixed = merge(z, [mine_ref[...], got_ref[...]])
        send_ref[...] = jnp.concatenate([mixed, stack_stats([highest, total])], axis=0).astype(BF16)


def final_merge_kernel(z, *refs):
    out_ref = refs[-1]
    _, total, mixed = merge(z, [ref[...] for ref in refs[:-1]])
    index = lax.broadcasted_iota(jnp.int32, (z.piece, 1), 0)
    out_ref[...] = (mixed / rows_to_column(total, index)).astype(BF16)


def pack_kernel(*refs):
    for i, ref in enumerate(refs[:-1]):
        refs[-1][i] = ref[...]


def share_order(groups):
    return list(range(groups - 1, -1, -1))


def output_products(z, weight_ref, sum_ref, pieces):
    me = lax.axis_index("ctx")
    for (d, first), (e, second) in zip(pieces[::2], pieces[1::2]):
        owners = [jnp.bitwise_xor(me, d), jnp.bitwise_xor(me, e)]
        weight = jnp.concatenate(
            [weight_ref[pl.ds(pl.multiple_of(x % z.heads * HD, HD), HD), :] for x in owners], axis=0
        )
        product = jnp.dot(
            jnp.concatenate([first[...], second[...]], axis=1), weight, preferred_element_type=F32
        )
        where = pl.ds(pl.multiple_of(owners[0] // z.heads * z.piece, 8), z.piece)
        sum_ref[where, :] = sum_ref[where, :] + product


def output_even_kernel(z, weight_ref, *refs):
    *piece_refs, sum_ref = refs
    sum_ref[...] = jnp.zeros_like(sum_ref)
    output_products(z, weight_ref, sum_ref, list(zip(range(0, z.n, 2), piece_refs)))


def output_odd_kernel(z, weight_ref, even_ref, first_ref, rest_ref, *refs):
    *out_refs, sum_ref = refs
    sum_ref[...] = even_ref[...]
    pieces = [(1, first_ref)] + [(2 * i + 3, rest_ref.at[i]) for i in range(z.n // 2 - 1)]
    output_products(z, weight_ref, sum_ref, pieces)
    place = lax.axis_index("kv")
    columns = sum_ref.shape[1]
    prompt_share = z.prompt // z.groups
    step_share = z.row_total // z.groups
    for out_ref, e in zip(out_refs, share_order(z.groups)):
        target = jnp.bitwise_xor(place, e)
        rows = [sum_ref[pl.ds(pl.multiple_of(target * prompt_share, 8), prompt_share), :]]
        for s in range(z.steps):
            start = z.prompt + s * z.row_total + target * step_share
            rows.append(sum_ref[pl.ds(pl.multiple_of(start, 8), step_share), :])
        share = jnp.concatenate(rows, axis=0)
        out_ref[...] = jnp.concatenate(
            [share[:, : columns // 2], share[:, columns // 2 :]], axis=0
        ).astype(BF16)


def share_sum_kernel(z, *refs):
    prompt_ref, step_ref = refs[z.groups :]
    total = refs[0][...].astype(F32)
    for ref in refs[1 : z.groups]:
        total = total + ref[...].astype(F32)
    prompt_share = z.prompt // z.groups
    step_share = z.row_total // z.groups
    half = total.shape[0] // 2
    columns = total.shape[1]
    for c in range(2):
        rows = total[c * half : (c + 1) * half]
        where = slice(c * columns, (c + 1) * columns)
        prompt_ref[:, where] = rows[0:prompt_share].astype(BF16)
        for s in range(z.steps):
            start = prompt_share + s * step_share
            step_ref[s, :, where] = rows[start : start + step_share].astype(BF16)


def swap(x, axis, size, d):
    return lax.ppermute(x, axis, [(i, i ^ d) for i in range(size)])


def on_device(
    prompt_in,
    step_in,
    norm_gain,
    query_weight,
    key_weight,
    value_weight,
    out_weight,
    key_cache,
    value_cache,
    cache_lengths,
    visible,
):
    n = lax.axis_size("ctx")
    groups = lax.axis_size("kv")
    z = Sizes(prompt_in, step_in, query_weight, visible, n, groups)
    pairs = n // 2

    cache_slots = key_cache.shape[1]
    cache = shape(cache_slots, HD, BF16)

    def prepare(lengths, seen):
        return call(
            functools.partial(prepare_kernel, z),
            [cache, cache, cache, shape(z.rows, z.slots, F32)],
            (lengths, seen.reshape(1, z.row_total), key_cache[0], value_cache[0]),
            "prepare",
            1e6,
            smem=1,
            far=2,
            scratch=[pltpu.SemaphoreType.DMA((2,))],
        )

    even, odd = call(
        functools.partial(project_kernel, z),
        [shape(z.project, HD, F32, pairs), shape(z.sent, HD, BF16, pairs)],
        (
            norm_gain.reshape(z.width // 128, 128),
            prompt_in,
            step_in.reshape(z.steps * z.row_total, z.width),
            query_weight,
            key_weight,
            value_weight,
        ),
        "project",
        2 * z.rows * z.width * (z.heads + 2) * HD,
        far=6,
        scratch=[
            pltpu.VMEM((z.width // 128, 128), BF16),
            pltpu.VMEM((z.prompt, z.width), BF16),
            pltpu.VMEM((z.steps * z.row_total, z.width), BF16),
            pltpu.VMEM((2, z.width // 2, z.heads * HD), BF16),
            pltpu.VMEM((z.width, HD), BF16),
            pltpu.VMEM((z.width, HD), BF16),
            pltpu.VMEM((z.rows, z.width), BF16),
            pltpu.VMEM((z.rows, z.heads * HD), F32),
            pltpu.VMEM((z.prompt, 2 * HD), F32),
            pltpu.VMEM((z.n * z.decode_slots, 2 * HD), F32),
            pltpu.SemaphoreType.DMA((7,)),
        ],
    )
    got = swap(odd, "ctx", n, 1)
    own, *sends = call(
        functools.partial(pair_sum_kernel, z),
        [shape(z.project, HD, F32)] + [shape(z.sent, HD, BF16)] * (pairs - 1),
        (even, got),
        "pair_sum",
        1e6,
    )
    visible, *sends = lax.optimization_barrier((visible, *sends))
    gots = [swap(send, "ctx", n, 2 * (i + 1)) for i, send in enumerate(sends)]
    keys, values, live, extra_bias = prepare(cache_lengths, visible)
    own, keys, values, live, extra_bias = lax.optimization_barrier(
        (own, keys, values, live, extra_bias)
    )
    query, extra_key, extra_value = call(
        functools.partial(finish_kernel, z, z.width * n),
        [shape(z.piece, HD, BF16), shape(z.slots, HD, BF16), shape(z.slots, HD, BF16)],
        (own, *gots),
        "finish",
        1e6,
    )

    queries = {1: swap(query, "ctx", n, 1)}
    for i in range(1, pairs):
        queries[2 * i] = swap(query, "ctx", n, 2 * i)

    def attend(pieces, stacked, name, packed=None, offset=None):
        message = shape(z.message, HD, BF16)
        outs = [shape(z.message, HD, BF16, len(pieces))] if stacked else [message] * len(pieces)
        return call(
            functools.partial(attention_kernel, z, pieces, stacked, offset),
            outs,
            (keys, values, live, extra_key, extra_value, extra_bias)
            + (tuple(queries[d] for d in pieces) if packed is None else (packed,)),
            name,
            8 * len(pieces) * z.piece * cache_slots * HD,
            )

    (first_odd,) = attend((1,), False, "attend_core")
    first_odd, *passed = lax.optimization_barrier(
        (first_odd, *[queries[2 * i] for i in range(1, pairs)])
    )
    for i in range(1, pairs):
        queries[2 * i] = passed[i - 1]
    packed = shape(z.piece, HD, BF16, pairs - 1)
    (relay,) = call(pack_kernel, [packed], tuple(passed), "pack_queries", 1e5)
    relayed = swap(relay, "ctx", n, 1)
    odd = [tuple(range(3, n, 2)[k : k + AT_ONCE]) for k in range(0, pairs - 1, AT_ONCE)]
    even = [(2,)] + [
        tuple(range(4, n, 2)[k : k + AT_ONCE]) for k in range(0, pairs - 2, AT_ONCE)
    ]
    early = attend(even[0], True, "attend_near")
    early, relayed = lax.optimization_barrier((early, relayed))
    rest_odd = [
        attend(pieces, True, f"attend_odd{k}", relayed, k * AT_ONCE)[0]
        for k, pieces in enumerate(odd)
    ]
    got_first = swap(first_odd, "ctx", n, 1)
    got_rest = [swap(block, "ctx", n, 1) for block in rest_odd]
    rest = list(early) + [
        attend(pieces, True, f"attend_even{k}")[0] for k, pieces in enumerate(even[1:])
    ]

    message = shape(z.message, HD, BF16)
    sends = call(
        functools.partial(
            pair_merge_kernel, z, [len(x) for x in even], [len(x) for x in odd]
        ),
        [message] * (pairs - 1),
        (*rest, *got_rest),
        "pair_merge",
        1e6,
    )
    query, *sends = lax.optimization_barrier((query, *sends))
    gots = [swap(send, "ctx", n, 2 * (i + 1)) for i, send in enumerate(sends)]
    queries[0] = query
    (own,) = attend((0,), False, "attend_own")
    (attended,) = call(
        functools.partial(final_merge_kernel, z),
        [shape(z.piece, HD, BF16)],
        (own, got_first, *gots),
        "final_merge",
        1e6,
    )
    even = [attended] + [swap(attended, "ctx", n, 2 * i) for i in range(1, pairs)]
    first_odd = swap(attended, "ctx", n, 1)
    (relay,) = call(pack_kernel, [packed], tuple(even[1:]), "pack_heads", 1e5)
    relay, *even = lax.optimization_barrier((relay, *even))
    rest_odd = swap(relay, "ctx", n, 1)

    columns = out_weight.shape[1]
    share_rows = 2 * z.rows // groups
    share = shape(share_rows, columns // 2, BF16)
    flops = z.rows * z.heads * HD * columns
    (total,) = call(
        functools.partial(output_even_kernel, z),
        [shape(z.rows, columns, F32)],
        (out_weight, *even),
        "output_even",
        flops,
    )
    shares = call(
        functools.partial(output_odd_kernel, z),
        [share] * groups,
        (out_weight, total, first_odd, rest_odd),
        "output_odd",
        flops,
        scratch=[pltpu.VMEM((z.rows, columns), F32)],
    )
    shares = [
        swap(x, "kv", groups, e) if e else x for x, e in zip(shares, share_order(groups))
    ]
    prompt_out, step_out = call(
        functools.partial(share_sum_kernel, z),
        [
            shape(z.prompt // groups, columns, BF16),
            shape(z.row_total // groups, columns, BF16, z.steps),
        ],
        tuple(shares),
        "share_sum",
        1e6,
    )
    return (prompt_out, step_out)


def solution(mesh):
    placed = (
        P(None, "ctx"),
        P(None, None, "ctx"),
        P("ctx"),
        P("ctx", "kv"),
        P("ctx", "kv"),
        P("ctx", "kv"),
        P("kv", "ctx"),
        P("kv", "ctx", None),
        P("kv", "ctx", None),
        P("ctx"),
        P(),
    )
    return jax.shard_map(
        on_device,
        mesh=mesh,
        in_specs=placed,
        out_specs=(P("kv", "ctx"), P(None, "kv", "ctx")),
        check_vma=False,
    )
```

```python
import functools

import jax
import jax.numpy as jnp
from jax import lax
from jax.experimental import pallas as pl
from jax.experimental.pallas import tpu as pltpu
from jax.sharding import PartitionSpec as P

HD = 128
EPSILON = 1e-05
MASKED = -1e30
LOG2E = 1.4426950408889634
SCALE = LOG2E / HD**0.5
STAT_ROWS = 16
AT_ONCE = 3
CHUNK = 1024
FIRST = 256
BLOCK = 512
TOO_LARGE = 2.0**60
VMEM_BYTES = 20 * 2**20
BF16 = jnp.bfloat16
F32 = jnp.float32


def up(count, multiple):
    return -(-count // multiple) * multiple


def split3(x):
    high = x.astype(BF16).astype(F32)
    rest = x - high
    middle = rest.astype(BF16).astype(F32)
    return high, middle, rest - middle


def pack_sums(z, total, squares):
    query = total[0 : z.piece]
    high = query.astype(BF16).astype(F32)
    return jnp.concatenate(
        [high, query - high, total[z.piece : z.body], stack_stats([squares])], axis=0
    ).astype(BF16)


def unpack_sums(z, sent):
    wide = sent.astype(F32)
    query = wide[0 : z.piece] + wide[z.piece : 2 * z.piece]
    total = jnp.concatenate([query, wide[2 * z.piece : z.piece + z.body]], axis=0)
    return total, read_stats(wide[z.piece + z.body :], z.square_lines, 1)[0]


def column_to_rows(column):
    count = column.shape[0]
    rows = []
    for start in range(0, count, 128):
        size = min(128, count - start)
        part = jnp.broadcast_to(column[start : start + size], (size, 128))
        on = lax.broadcasted_iota(jnp.int32, (size, 128), 0) == lax.broadcasted_iota(
            jnp.int32, (size, 128), 1
        )
        rows.append(jnp.sum(jnp.where(on, part, 0.0), axis=0, keepdims=True))
    return jnp.concatenate(rows, axis=0)


def rows_to_column(rows, index):
    total = 0.0
    for k in range(rows.shape[0]):
        lanes = lax.broadcasted_iota(jnp.int32, (index.shape[0], 128), 1) + 128 * k
        total = total + jnp.sum(
            jnp.where(lanes == index, rows[k : k + 1, :], 0.0), axis=1, keepdims=True
        )
    return total


def stack_stats(rows_list):
    parts = []
    for rows in rows_list:
        parts.extend(split3(rows))
    used = sum(part.shape[0] for part in parts)
    parts.append(jnp.zeros((STAT_ROWS - used, 128), F32))
    return jnp.concatenate(parts, axis=0)


def read_stats(block, count, kinds):
    out = []
    for kind in range(kinds):
        base = kind * 3 * count
        out.append(
            block[base : base + count]
            + block[base + count : base + 2 * count]
            + block[base + 2 * count : base + 3 * count]
        )
    return out


def call(kernel, out_shape, args, name, flops, smem=0, far=0, grant=VMEM_BYTES, scratch=()):
    whole = pl.BlockSpec(memory_space=pltpu.VMEM)
    scalar = pl.BlockSpec(memory_space=pltpu.SMEM)
    near = len(args) - far
    args = args[:near] + tuple(
        pltpu.with_memory_space_constraint(x, pltpu.HBM) for x in args[near:]
    )
    return pl.pallas_call(
        kernel,
        out_shape=out_shape,
        in_specs=[scalar] * smem
        + [whole] * (near - smem)
        + [pl.BlockSpec(memory_space=pltpu.HBM)] * far,
        out_specs=jax.tree.map(lambda _: whole, out_shape),
        scratch_shapes=list(scratch),
        compiler_params=pltpu.CompilerParams(vmem_limit_bytes=grant),
        cost_estimate=pl.CostEstimate(
            flops=int(flops), bytes_accessed=1 << 20, transcendentals=0
        ),
        name=name,
    )(*args)


def shape(rows, columns, dtype, *lead):
    return jax.ShapeDtypeStruct(tuple(lead) + (rows, columns), dtype)


class Sizes:
    def __init__(self, prompt_in, step_in, query_weight, visible, devices, groups):
        self.n = devices
        self.groups = groups
        self.prompt = prompt_in.shape[0]
        self.steps = step_in.shape[0]
        self.row_total = visible.shape[0]
        self.rows = self.prompt + self.steps * self.row_total
        self.width = prompt_in.shape[1]
        self.heads = query_weight.shape[1] // HD
        self.halves = devices // self.heads
        self.piece = self.rows // self.halves
        self.stat_lines = up(self.piece, 128) // 128
        self.square_lines = up(self.rows, 128) // 128
        self.prompt_own = self.prompt // devices
        self.rows_own = self.row_total // devices
        self.decode_own = self.rows_own * self.steps
        self.decode_slots = up(self.decode_own, 16)
        self.prompt_slots = up(self.prompt_own, 16)
        self.slots = self.prompt_slots + self.decode_slots
        self.message = self.piece + STAT_ROWS
        self.body = self.piece + 2 * self.slots
        self.project = self.body + STAT_ROWS
        self.sent = self.piece + self.project


def project_kernel(z, gain_hbm, xp_hbm, xs_hbm, wq_hbm, wk_hbm, wv_hbm, even_ref, odd_ref, gain_ref, xp_ref, xs_ref, wq_ref, wk_ref, wv_ref, scaled_ref, query_ref, kvp_ref, kvd_ref, sems):
    me = lax.axis_index("ctx")
    depth = z.width // 2
    loads = [
        pltpu.make_async_copy(xp_hbm, xp_ref, sems.at[0]),
        pltpu.make_async_copy(xs_hbm, xs_ref, sems.at[1]),
        pltpu.make_async_copy(wk_hbm, wk_ref, sems.at[2]),
        pltpu.make_async_copy(wv_hbm, wv_ref, sems.at[3]),
    ]
    loads += [
        pltpu.make_async_copy(wq_hbm.at[pl.ds(k * depth, depth), :], wq_ref.at[k], sems.at[4 + k])
        for k in range(2)
    ]
    loads.append(pltpu.make_async_copy(gain_hbm, gain_ref, sems.at[6]))
    loads[6].start()
    for load in loads[:6]:
        load.start()
    loads[6].wait()
    gain = gain_ref[...].astype(F32)
    gain = jnp.concatenate([gain[k : k + 1, :] for k in range(gain.shape[0])], axis=1)
    squares = []
    for k, (ref, base, size) in enumerate(
        (
            (xp_ref, 0, z.prompt),
            (xs_ref, z.prompt, z.steps * z.row_total),
        )
    ):
        loads[k].wait()
        wide = ref[...].astype(F32)
        squares.append(jnp.sum(wide * wide, axis=1, keepdims=True))
        scaled_ref[base : base + size, :] = (wide * gain).astype(BF16)
    square_rows = column_to_rows(jnp.concatenate(squares, axis=0))
    pad = jnp.zeros((STAT_ROWS - z.square_lines, 128), F32)
    decode = z.steps * z.row_total
    count = z.n * z.decode_slots
    place = lax.broadcasted_iota(jnp.int32, (count, decode), 0)
    source = lax.broadcasted_iota(jnp.int32, (count, decode), 1)
    slot = place % z.decode_slots
    wanted = (
        (slot // z.rows_own) * z.row_total
        + (place // z.decode_slots) * z.rows_own
        + slot % z.rows_own
    )
    pick = ((wanted == source) & (slot < z.decode_own)).astype(F32).astype(BF16)
    ordered = jnp.dot(
        pick, scaled_ref[z.prompt : z.rows, :], preferred_element_type=F32
    ).astype(BF16)
    for c, ref in enumerate((wk_ref, wv_ref)):
        loads[2 + c].wait()
        kvp_ref[:, c * HD : (c + 1) * HD] = jnp.dot(
            scaled_ref[0 : z.prompt, :], ref[...], preferred_element_type=F32
        )
        kvd_ref[:, c * HD : (c + 1) * HD] = jnp.dot(ordered, ref[...], preferred_element_type=F32)
    loads[4].wait()
    product = jnp.dot(scaled_ref[:, :depth], wq_ref[0], preferred_element_type=F32)
    loads[5].wait()
    query_ref[...] = product + jnp.dot(
        scaled_ref[:, depth:], wq_ref[1], preferred_element_type=F32
    )
    for d in range(z.n):
        owner = jnp.bitwise_xor(me, d)
        half = owner // z.heads
        part = query_ref[
            pl.ds(pl.multiple_of(half * z.piece, 8), z.piece),
            pl.ds(pl.multiple_of(owner % z.heads * HD, HD), HD),
        ]
        kvp = kvp_ref[pl.ds(pl.multiple_of(owner * z.prompt_own, 8), z.prompt_own), :]
        kvd = kvd_ref[pl.ds(pl.multiple_of(owner * z.decode_slots, 8), z.decode_slots), :]
        total = jnp.concatenate([part, kvp[:, :HD], kvd[:, :HD], kvp[:, HD:], kvd[:, HD:]], axis=0)
        if d % 2:
            odd_ref[d // 2] = pack_sums(z, total, square_rows)
        else:
            even_ref[d // 2] = jnp.concatenate([total, square_rows, pad], axis=0)


def pair_sum_kernel(z, even_ref, got_ref, own_ref, *send_refs):
    for i in range(z.n // 2):
        total, squares = unpack_sums(z, got_ref[i])
        total = total + even_ref[i, 0 : z.body, :]
        squares = squares + even_ref[i, z.body : z.body + z.square_lines, :]
        if i == 0:
            pad = jnp.zeros((STAT_ROWS - z.square_lines, 128), F32)
            own_ref[...] = jnp.concatenate([total, squares, pad], axis=0)
        else:
            send_refs[i - 1][...] = pack_sums(z, total, squares)


def finish_kernel(z, features, own_ref, *refs):
    got_refs = refs[: z.n // 2 - 1]
    query_ref, key_ref, value_ref = refs[z.n // 2 - 1 :]
    me = lax.axis_index("ctx")
    total = own_ref[0 : z.body, :]
    squares = own_ref[z.body : z.body + z.square_lines, :]
    for ref in got_refs:
        got, got_squares = unpack_sums(z, ref[...])
        total = total + got
        squares = squares + got_squares
    inverse = lax.rsqrt(squares / features + EPSILON)
    rows = lax.broadcasted_iota(jnp.int32, (z.piece, 1), 0) + (me // z.heads) * z.piece
    query_ref[...] = (total[0 : z.piece] * rows_to_column(inverse, rows)).astype(BF16)
    slot = lax.broadcasted_iota(jnp.int32, (z.slots, 1), 0)
    late = slot - z.prompt_slots
    index = jnp.where(
        slot < z.prompt_slots,
        me * z.prompt_own + slot,
        z.prompt
        + (late // z.rows_own) * z.row_total
        + me * z.rows_own
        + late % z.rows_own,
    )
    own = rows_to_column(inverse, index)
    key_ref[...] = (total[z.piece : z.piece + z.slots] * own).astype(BF16)
    value_ref[...] = (total[z.piece + z.slots : z.piece + 2 * z.slots] * own).astype(BF16)


def prepare_kernel(z, length_ref, visible_ref, key_hbm, value_hbm, key_ref, value_ref, live_ref, extra_ref, sems):
    loads = [
        pltpu.make_async_copy(key_hbm, key_ref, sems.at[0]),
        pltpu.make_async_copy(value_hbm, value_ref, sems.at[1]),
    ]
    for load in loads:
        load.start()
    me = lax.axis_index("ctx")
    length = length_ref[0]
    size = min(BLOCK, key_ref.shape[0])
    blocks = key_ref.shape[0] // size
    local = lax.broadcasted_iota(jnp.int32, (size, HD), 0)

    def mark(i, carry):
        rows = pl.ds(pl.multiple_of(i * size, size), size)
        live_ref[rows, :] = jnp.where(local + i * size < length, 1.0, 0.0).astype(BF16)
        return carry

    lax.fori_loop(0, blocks, mark, 0)
    row = lax.broadcasted_iota(jnp.int32, (z.rows, 1), 0)
    late = row - z.prompt
    step = late // z.row_total
    place = late - step * z.row_total
    lanes = lax.broadcasted_iota(jnp.int32, (z.rows, z.row_total), 1)
    allowed = jnp.sum(
        jnp.where(lanes == place, visible_ref[...].astype(F32), 0.0), axis=1, keepdims=True
    )
    limit = jnp.where(late < 0, row + 1, allowed.astype(jnp.int32))
    slot = lax.broadcasted_iota(jnp.int32, (z.rows, z.slots), 1)
    late_slot = slot - z.prompt_slots
    from_prompt = (slot < z.prompt_own) & (me * z.prompt_own + slot < limit)
    from_decode = (
        (late_slot >= 0)
        & (late_slot < z.decode_own)
        & (late >= 0)
        & (me * z.rows_own + late_slot % z.rows_own == place)
        & (late_slot // z.rows_own <= step)
    )
    extra_ref[...] = jnp.where(from_prompt | from_decode, 0.0, MASKED)
    for load in loads:
        load.wait()
    stand_in = jnp.broadcast_to(key_ref[0:16, :].astype(F32)[0:1, :], (size, HD))

    def clear(i, carry):
        rows = pl.ds(pl.multiple_of(i * size, size), size)
        live = local + i * size < length
        key_ref[rows, :] = jnp.where(live, key_ref[rows, :].astype(F32), stand_in).astype(BF16)
        value_ref[rows, :] = jnp.where(live, value_ref[rows, :].astype(F32), 0.0).astype(BF16)
        return carry

    lax.fori_loop(length // size, blocks, clear, 0)


def beside(values, live):
    return jnp.concatenate([values, live], axis=1)


def attention_kernel(z, pieces, stacked, offset, *refs):
    key_ref, value_ref, live_ref, extra_key_ref, extra_value_ref, extra_bias_ref = refs[:6]
    if offset is None:
        query_refs = refs[6 : 6 + len(pieces)]
        out_refs = refs[6 + len(pieces) :]
    else:
        query_refs = [refs[6].at[offset + i] for i in range(len(pieces))]
        out_refs = refs[7:]
    me = lax.axis_index("ctx")
    over = (((1,), (1,)), ((), ()))
    slots = key_ref.shape[0]

    def scores(query, rows):
        return lax.dot_general(query, key_ref[rows, :], over, preferred_element_type=F32)

    def mix(weight, rows):
        return jnp.dot(
            weight.astype(BF16), beside(value_ref[rows, :], live_ref[rows, :]),
            preferred_element_type=F32,
        )

    def extras(query, d):
        half = jnp.bitwise_xor(me, d) // z.heads
        bias = extra_bias_ref[pl.ds(pl.multiple_of(half * z.piece, 8), z.piece), :]
        score = lax.dot_general(query, extra_key_ref[...], over, preferred_element_type=F32)
        return score + bias

    def mix_extras(weight):
        ones = jnp.ones((z.slots, HD), BF16)
        return jnp.dot(
            weight.astype(BF16), beside(extra_value_ref[...], ones), preferred_element_type=F32
        )

    def write(i, level, mixed):
        stats = stack_stats([column_to_rows(level * SCALE), column_to_rows(mixed[:, HD : HD + 1])])
        message = jnp.concatenate([mixed[:, :HD], stats], axis=0).astype(BF16)
        if stacked:
            out_refs[0][i] = message
        else:
            out_refs[i][...] = message

    first = min(FIRST, slots)
    chunk = min(CHUNK, slots)
    bounds = [0, first] + [k for k in range(chunk, slots + 1, chunk) if k > first]
    worst = None
    for i, d in enumerate(pieces):
        query = query_refs[i][...]
        score = scores(query, slice(0, first))
        level = jnp.max(score, axis=1, keepdims=True)
        mixed = mix(jnp.exp2((score - level) * SCALE), slice(0, first))
        for start, end in zip(bounds[1:], bounds[2:]):
            rows = slice(start, end)
            mixed = mixed + mix(jnp.exp2((scores(query, rows) - level) * SCALE), rows)
        mixed = mixed + mix_extras(jnp.exp2((extras(query, d) - level) * SCALE))
        write(i, level, mixed)
        over_limit = jnp.where(mixed[:, HD:] < TOO_LARGE, 0.0, 1.0)
        worst = over_limit if worst is None else jnp.maximum(worst, over_limit)

    @pl.when(jnp.max(worst) > 0.0)
    def _():
        for i, d in enumerate(pieces):
            query = query_refs[i][...]
            score = extras(query, d)
            level = jnp.max(score, axis=1, keepdims=True)
            mixed = mix_extras(jnp.exp2((score - level) * SCALE))

            def step(k, carry):
                level, mixed = carry
                rows = pl.ds(pl.multiple_of(k * chunk, chunk), chunk)
                score = scores(query, rows)
                higher = jnp.maximum(level, jnp.max(score, axis=1, keepdims=True))
                return higher, mixed * jnp.exp2((level - higher) * SCALE) + mix(
                    jnp.exp2((score - higher) * SCALE), rows
                )

            level, mixed = lax.fori_loop(0, slots // chunk, step, (level, mixed))
            write(i, level, mixed)


def merge(z, messages):
    blocks = []
    for message in messages:
        wide = message.astype(F32)
        top, total = read_stats(wide[z.piece :], z.stat_lines, 2)
        blocks.append((top, total, wide[0 : z.piece]))
    highest = functools.reduce(jnp.maximum, [top for top, _, _ in blocks])
    index = lax.broadcasted_iota(jnp.int32, (z.piece, 1), 0)
    total = 0.0
    mixed = 0.0
    for top, block_total, block_mixed in blocks:
        scale = jnp.exp2(top - highest)
        total = total + block_total * scale
        mixed = mixed + block_mixed * rows_to_column(scale, index)
    return highest, total, mixed


def pair_merge_kernel(z, mine_sets, got_sets, *refs):
    count = len(mine_sets) + len(got_sets)
    places = [
        [ref.at[k] for ref, size in zip(block, sizes) for k in range(size)]
        for block, sizes in ((refs, mine_sets), (refs[len(mine_sets) :], got_sets))
    ]
    for send_ref, mine_ref, got_ref in zip(refs[count:], *places):
        highest, total, mixed = merge(z, [mine_ref[...], got_ref[...]])
        send_ref[...] = jnp.concatenate([mixed, stack_stats([highest, total])], axis=0).astype(BF16)


def final_merge_kernel(z, *refs):
    out_ref = refs[-1]
    _, total, mixed = merge(z, [ref[...] for ref in refs[:-1]])
    index = lax.broadcasted_iota(jnp.int32, (z.piece, 1), 0)
    out_ref[...] = (mixed / rows_to_column(total, index)).astype(BF16)


def pack_kernel(*refs):
    for i, ref in enumerate(refs[:-1]):
        refs[-1][i] = ref[...]


def share_order(groups):
    return list(range(2, groups)) + [1, 0]


def output_products(z, weight_ref, sum_ref, pieces):
    me = lax.axis_index("ctx")
    for (d, first), (e, second) in zip(pieces[::2], pieces[1::2]):
        owners = [jnp.bitwise_xor(me, d), jnp.bitwise_xor(me, e)]
        weight = jnp.concatenate(
            [weight_ref[pl.ds(pl.multiple_of(x % z.heads * HD, HD), HD), :] for x in owners], axis=0
        )
        product = jnp.dot(
            jnp.concatenate([first[...], second[...]], axis=1), weight, preferred_element_type=F32
        )
        where = pl.ds(pl.multiple_of(owners[0] // z.heads * z.piece, 8), z.piece)
        sum_ref[where, :] = sum_ref[where, :] + product


def output_even_kernel(z, weight_ref, *refs):
    *piece_refs, sum_ref = refs
    sum_ref[...] = jnp.zeros_like(sum_ref)
    output_products(z, weight_ref, sum_ref, list(zip(range(0, z.n, 2), piece_refs)))


def output_odd_kernel(z, weight_ref, even_ref, first_ref, rest_ref, *refs):
    *out_refs, sum_ref = refs
    sum_ref[...] = even_ref[...]
    pieces = [(1, first_ref)] + [(2 * i + 3, rest_ref.at[i]) for i in range(z.n // 2 - 1)]
    output_products(z, weight_ref, sum_ref, pieces)
    place = lax.axis_index("kv")
    columns = sum_ref.shape[1]
    prompt_share = z.prompt // z.groups
    step_share = z.row_total // z.groups
    for out_ref, e in zip(out_refs, share_order(z.groups)):
        target = jnp.bitwise_xor(place, e)
        rows = [sum_ref[pl.ds(pl.multiple_of(target * prompt_share, 8), prompt_share), :]]
        for s in range(z.steps):
            start = z.prompt + s * z.row_total + target * step_share
            rows.append(sum_ref[pl.ds(pl.multiple_of(start, 8), step_share), :])
        share = jnp.concatenate(rows, axis=0)
        out_ref[...] = jnp.concatenate(
            [share[:, : columns // 2], share[:, columns // 2 :]], axis=0
        ).astype(BF16)


def share_sum_kernel(z, *refs):
    prompt_ref, step_ref = refs[z.groups :]
    total = refs[0][...].astype(F32)
    for ref in refs[1 : z.groups]:
        total = total + ref[...].astype(F32)
    prompt_share = z.prompt // z.groups
    step_share = z.row_total // z.groups
    half = total.shape[0] // 2
    columns = total.shape[1]
    for c in range(2):
        rows = total[c * half : (c + 1) * half]
        where = slice(c * columns, (c + 1) * columns)
        prompt_ref[:, where] = rows[0:prompt_share].astype(BF16)
        for s in range(z.steps):
            start = prompt_share + s * step_share
            step_ref[s, :, where] = rows[start : start + step_share].astype(BF16)


def swap(x, axis, size, d):
    return lax.ppermute(x, axis, [(i, i ^ d) for i in range(size)])


def on_device(
    prompt_in,
    step_in,
    norm_gain,
    query_weight,
    key_weight,
    value_weight,
    out_weight,
    key_cache,
    value_cache,
    cache_lengths,
    visible,
):
    n = lax.axis_size("ctx")
    groups = lax.axis_size("kv")
    z = Sizes(prompt_in, step_in, query_weight, visible, n, groups)
    pairs = n // 2

    cache_slots = key_cache.shape[1]
    cache = shape(cache_slots, HD, BF16)

    def prepare(lengths, seen):
        return call(
            functools.partial(prepare_kernel, z),
            [cache, cache, cache, shape(z.rows, z.slots, F32)],
            (lengths, seen.reshape(1, z.row_total), key_cache[0], value_cache[0]),
            "prepare",
            1e6,
            smem=1,
            far=2,
            scratch=[pltpu.SemaphoreType.DMA((2,))],
        )

    even, odd = call(
        functools.partial(project_kernel, z),
        [shape(z.project, HD, F32, pairs), shape(z.sent, HD, BF16, pairs)],
        (
            norm_gain.reshape(z.width // 128, 128),
            prompt_in,
            step_in.reshape(z.steps * z.row_total, z.width),
            query_weight,
            key_weight,
            value_weight,
        ),
        "project",
        2 * z.rows * z.width * (z.heads + 2) * HD,
        far=6,
        scratch=[
            pltpu.VMEM((z.width // 128, 128), BF16),
            pltpu.VMEM((z.prompt, z.width), BF16),
            pltpu.VMEM((z.steps * z.row_total, z.width), BF16),
            pltpu.VMEM((2, z.width // 2, z.heads * HD), BF16),
            pltpu.VMEM((z.width, HD), BF16),
            pltpu.VMEM((z.width, HD), BF16),
            pltpu.VMEM((z.rows, z.width), BF16),
            pltpu.VMEM((z.rows, z.heads * HD), F32),
            pltpu.VMEM((z.prompt, 2 * HD), F32),
            pltpu.VMEM((z.n * z.decode_slots, 2 * HD), F32),
            pltpu.SemaphoreType.DMA((7,)),
        ],
    )
    got = swap(odd, "ctx", n, 1)
    own, *sends = call(
        functools.partial(pair_sum_kernel, z),
        [shape(z.project, HD, F32)] + [shape(z.sent, HD, BF16)] * (pairs - 1),
        (even, got),
        "pair_sum",
        1e6,
    )
    visible, *sends = lax.optimization_barrier((visible, *sends))
    gots = [swap(send, "ctx", n, 2 * (i + 1)) for i, send in enumerate(sends)]
    keys, values, live, extra_bias = prepare(cache_lengths, visible)
    own, keys, values, live, extra_bias = lax.optimization_barrier(
        (own, keys, values, live, extra_bias)
    )
    query, extra_key, extra_value = call(
        functools.partial(finish_kernel, z, z.width * n),
        [shape(z.piece, HD, BF16), shape(z.slots, HD, BF16), shape(z.slots, HD, BF16)],
        (own, *gots),
        "finish",
        1e6,
    )

    queries = {1: swap(query, "ctx", n, 1)}
    for i in range(1, pairs):
        queries[2 * i] = swap(query, "ctx", n, 2 * i)

    def attend(pieces, stacked, name, packed=None, offset=None):
        message = shape(z.message, HD, BF16)
        outs = [shape(z.message, HD, BF16, len(pieces))] if stacked else [message] * len(pieces)
        return call(
            functools.partial(attention_kernel, z, pieces, stacked, offset),
            outs,
            (keys, values, live, extra_key, extra_value, extra_bias)
            + (tuple(queries[d] for d in pieces) if packed is None else (packed,)),
            name,
            8 * len(pieces) * z.piece * cache_slots * HD,
            )

    (first_odd,) = attend((1,), False, "attend_core")
    first_odd, *passed = lax.optimization_barrier(
        (first_odd, *[queries[2 * i] for i in range(1, pairs)])
    )
    for i in range(1, pairs):
        queries[2 * i] = passed[i - 1]
    packed = shape(z.piece, HD, BF16, pairs - 1)
    (relay,) = call(pack_kernel, [packed], tuple(passed), "pack_queries", 1e5)
    relayed = swap(relay, "ctx", n, 1)
    odd = [tuple(range(3, n, 2)[k : k + AT_ONCE]) for k in range(0, pairs - 1, AT_ONCE)]
    even = [(2,)] + [
        tuple(range(4, n, 2)[k : k + AT_ONCE]) for k in range(0, pairs - 2, AT_ONCE)
    ]
    early = attend(even[0], True, "attend_near")
    early, relayed = lax.optimization_barrier((early, relayed))
    rest_odd = [
        attend(pieces, True, f"attend_odd{k}", relayed, k * AT_ONCE)[0]
        for k, pieces in enumerate(odd)
    ]
    got_first = swap(first_odd, "ctx", n, 1)
    got_rest = [swap(block, "ctx", n, 1) for block in rest_odd]
    rest = list(early) + [
        attend(pieces, True, f"attend_even{k}")[0] for k, pieces in enumerate(even[1:])
    ]

    message = shape(z.message, HD, BF16)
    sends = call(
        functools.partial(
            pair_merge_kernel, z, [len(x) for x in even], [len(x) for x in odd]
        ),
        [message] * (pairs - 1),
        (*rest, *got_rest),
        "pair_merge",
        1e6,
    )
    query, *sends = lax.optimization_barrier((query, *sends))
    gots = [swap(send, "ctx", n, 2 * (i + 1)) for i, send in enumerate(sends)]
    queries[0] = query
    (own,) = attend((0,), False, "attend_own")
    (attended,) = call(
        functools.partial(final_merge_kernel, z),
        [shape(z.piece, HD, BF16)],
        (own, got_first, *gots),
        "final_merge",
        1e6,
    )
    even = [attended] + [swap(attended, "ctx", n, 2 * i) for i in range(1, pairs)]
    first_odd = swap(attended, "ctx", n, 1)
    (relay,) = call(pack_kernel, [packed], tuple(even[1:]), "pack_heads", 1e5)
    relay, *even = lax.optimization_barrier((relay, *even))
    rest_odd = swap(relay, "ctx", n, 1)

    columns = out_weight.shape[1]
    share_rows = 2 * z.rows // groups
    share = shape(share_rows, columns // 2, BF16)
    flops = z.rows * z.heads * HD * columns
    (total,) = call(
        functools.partial(output_even_kernel, z),
        [shape(z.rows, columns, F32)],
        (out_weight, *even),
        "output_even",
        flops,
    )
    shares = call(
        functools.partial(output_odd_kernel, z),
        [share] * groups,
        (out_weight, total, first_odd, rest_odd),
        "output_odd",
        flops,
        scratch=[pltpu.VMEM((z.rows, columns), F32)],
    )
    shares = [
        swap(x, "kv", groups, e) if e else x for x, e in zip(shares, share_order(groups))
    ]
    prompt_out, step_out = call(
        functools.partial(share_sum_kernel, z),
        [
            shape(z.prompt // groups, columns, BF16),
            shape(z.row_total // groups, columns, BF16, z.steps),
        ],
        tuple(shares),
        "share_sum",
        1e6,
    )
    return (prompt_out, step_out)


def solution(mesh):
    placed = (
        P(None, "ctx"),
        P(None, None, "ctx"),
        P("ctx"),
        P("ctx", "kv"),
        P("ctx", "kv"),
        P("ctx", "kv"),
        P("kv", "ctx"),
        P("kv", "ctx", None),
        P("kv", "ctx", None),
        P("ctx"),
        P(),
    )
    return jax.shard_map(
        on_device,
        mesh=mesh,
        in_specs=placed,
        out_specs=(P("kv", "ctx"), P(None, "kv", "ctx")),
        check_vma=False,
    )
```

```python
import functools

import jax
import jax.numpy as jnp
from jax import lax
from jax.experimental import pallas as pl
from jax.experimental.pallas import tpu as pltpu
from jax.sharding import PartitionSpec as P

HD = 128
EPSILON = 1e-05
MASKED = -1e30
LOG2E = 1.4426950408889634
SCALE = LOG2E / HD**0.5
STAT_ROWS = 16
AT_ONCE = 3
CHUNK = 1024
FIRST = 256
BLOCK = 512
TOO_LARGE = 2.0**60
VMEM_BYTES = 20 * 2**20
BF16 = jnp.bfloat16
F32 = jnp.float32


def up(count, multiple):
    return -(-count // multiple) * multiple


def split3(x):
    high = x.astype(BF16).astype(F32)
    rest = x - high
    middle = rest.astype(BF16).astype(F32)
    return high, middle, rest - middle


def pack_sums(z, total, squares):
    query = total[0 : z.piece]
    high = query.astype(BF16).astype(F32)
    return jnp.concatenate(
        [high, query - high, total[z.piece : z.body], stack_stats([squares])], axis=0
    ).astype(BF16)


def unpack_sums(z, sent):
    wide = sent.astype(F32)
    query = wide[0 : z.piece] + wide[z.piece : 2 * z.piece]
    total = jnp.concatenate([query, wide[2 * z.piece : z.piece + z.body]], axis=0)
    return total, read_stats(wide[z.piece + z.body :], z.square_lines, 1)[0]


def column_to_rows(column):
    count = column.shape[0]
    rows = []
    for start in range(0, count, 128):
        size = min(128, count - start)
        part = jnp.broadcast_to(column[start : start + size], (size, 128))
        on = lax.broadcasted_iota(jnp.int32, (size, 128), 0) == lax.broadcasted_iota(
            jnp.int32, (size, 128), 1
        )
        rows.append(jnp.sum(jnp.where(on, part, 0.0), axis=0, keepdims=True))
    return jnp.concatenate(rows, axis=0)


def rows_to_column(rows, index):
    total = 0.0
    for k in range(rows.shape[0]):
        lanes = lax.broadcasted_iota(jnp.int32, (index.shape[0], 128), 1) + 128 * k
        total = total + jnp.sum(
            jnp.where(lanes == index, rows[k : k + 1, :], 0.0), axis=1, keepdims=True
        )
    return total


def stack_stats(rows_list):
    parts = []
    for rows in rows_list:
        parts.extend(split3(rows))
    used = sum(part.shape[0] for part in parts)
    parts.append(jnp.zeros((STAT_ROWS - used, 128), F32))
    return jnp.concatenate(parts, axis=0)


def read_stats(block, count, kinds):
    out = []
    for kind in range(kinds):
        base = kind * 3 * count
        out.append(
            block[base : base + count]
            + block[base + count : base + 2 * count]
            + block[base + 2 * count : base + 3 * count]
        )
    return out


def call(kernel, out_shape, args, name, flops, smem=0, far=0, grant=VMEM_BYTES, scratch=()):
    whole = pl.BlockSpec(memory_space=pltpu.VMEM)
    scalar = pl.BlockSpec(memory_space=pltpu.SMEM)
    near = len(args) - far
    args = args[:near] + tuple(
        pltpu.with_memory_space_constraint(x, pltpu.HBM) for x in args[near:]
    )
    return pl.pallas_call(
        kernel,
        out_shape=out_shape,
        in_specs=[scalar] * smem
        + [whole] * (near - smem)
        + [pl.BlockSpec(memory_space=pltpu.HBM)] * far,
        out_specs=jax.tree.map(lambda _: whole, out_shape),
        scratch_shapes=list(scratch),
        compiler_params=pltpu.CompilerParams(vmem_limit_bytes=grant),
        cost_estimate=pl.CostEstimate(
            flops=int(flops), bytes_accessed=1 << 20, transcendentals=0
        ),
        name=name,
    )(*args)


def shape(rows, columns, dtype, *lead):
    return jax.ShapeDtypeStruct(tuple(lead) + (rows, columns), dtype)


class Sizes:
    def __init__(self, prompt_in, step_in, query_weight, visible, devices, groups):
        self.n = devices
        self.groups = groups
        self.prompt = prompt_in.shape[0]
        self.steps = step_in.shape[0]
        self.row_total = visible.shape[0]
        self.rows = self.prompt + self.steps * self.row_total
        self.width = prompt_in.shape[1]
        self.heads = query_weight.shape[1] // HD
        self.halves = devices // self.heads
        self.piece = self.rows // self.halves
        self.stat_lines = up(self.piece, 128) // 128
        self.square_lines = up(self.rows, 128) // 128
        self.prompt_own = self.prompt // devices
        self.rows_own = self.row_total // devices
        self.decode_own = self.rows_own * self.steps
        self.decode_slots = up(self.decode_own, 16)
        self.prompt_slots = up(self.prompt_own, 16)
        self.slots = self.prompt_slots + self.decode_slots
        self.message = self.piece + STAT_ROWS
        self.body = self.piece + 2 * self.slots
        self.project = self.body + STAT_ROWS
        self.sent = self.piece + self.project


def project_kernel(z, gain_hbm, xp_hbm, xs_hbm, wq_hbm, wk_hbm, wv_hbm, even_ref, odd_ref, gain_ref, xp_ref, xs_ref, wq_ref, wk_ref, wv_ref, scaled_ref, query_ref, kvp_ref, kvd_ref, sems):
    me = lax.axis_index("ctx")
    depth = z.width // 2
    loads = [
        pltpu.make_async_copy(xp_hbm, xp_ref, sems.at[0]),
        pltpu.make_async_copy(xs_hbm, xs_ref, sems.at[1]),
        pltpu.make_async_copy(wk_hbm, wk_ref, sems.at[2]),
        pltpu.make_async_copy(wv_hbm, wv_ref, sems.at[3]),
    ]
    loads += [
        pltpu.make_async_copy(wq_hbm.at[pl.ds(k * depth, depth), :], wq_ref.at[k], sems.at[4 + k])
        for k in range(2)
    ]
    loads.append(pltpu.make_async_copy(gain_hbm, gain_ref, sems.at[6]))
    loads[6].start()
    for load in loads[:6]:
        load.start()
    loads[6].wait()
    gain = gain_ref[...].astype(F32)
    gain = jnp.concatenate([gain[k : k + 1, :] for k in range(gain.shape[0])], axis=1)
    squares = []
    for k, (ref, base, size) in enumerate(
        (
            (xp_ref, 0, z.prompt),
            (xs_ref, z.prompt, z.steps * z.row_total),
        )
    ):
        loads[k].wait()
        wide = ref[...].astype(F32)
        squares.append(jnp.sum(wide * wide, axis=1, keepdims=True))
        scaled_ref[base : base + size, :] = (wide * gain).astype(BF16)
    square_rows = column_to_rows(jnp.concatenate(squares, axis=0))
    pad = jnp.zeros((STAT_ROWS - z.square_lines, 128), F32)
    decode = z.steps * z.row_total
    count = z.n * z.decode_slots
    place = lax.broadcasted_iota(jnp.int32, (count, decode), 0)
    source = lax.broadcasted_iota(jnp.int32, (count, decode), 1)
    slot = place % z.decode_slots
    wanted = (
        (slot // z.rows_own) * z.row_total
        + (place // z.decode_slots) * z.rows_own
        + slot % z.rows_own
    )
    pick = ((wanted == source) & (slot < z.decode_own)).astype(F32).astype(BF16)
    ordered = jnp.dot(
        pick, scaled_ref[z.prompt : z.rows, :], preferred_element_type=F32
    ).astype(BF16)
    for c, ref in enumerate((wk_ref, wv_ref)):
        loads[2 + c].wait()
        kvp_ref[:, c * HD : (c + 1) * HD] = jnp.dot(
            scaled_ref[0 : z.prompt, :], ref[...], preferred_element_type=F32
        )
        kvd_ref[:, c * HD : (c + 1) * HD] = jnp.dot(ordered, ref[...], preferred_element_type=F32)
    loads[4].wait()
    product = jnp.dot(scaled_ref[:, :depth], wq_ref[0], preferred_element_type=F32)
    loads[5].wait()
    query_ref[...] = product + jnp.dot(
        scaled_ref[:, depth:], wq_ref[1], preferred_element_type=F32
    )
    for d in range(z.n):
        owner = jnp.bitwise_xor(me, d)
        half = owner // z.heads
        part = query_ref[
            pl.ds(pl.multiple_of(half * z.piece, 8), z.piece),
            pl.ds(pl.multiple_of(owner % z.heads * HD, HD), HD),
        ]
        kvp = kvp_ref[pl.ds(pl.multiple_of(owner * z.prompt_own, 8), z.prompt_own), :]
        kvd = kvd_ref[pl.ds(pl.multiple_of(owner * z.decode_slots, 8), z.decode_slots), :]
        total = jnp.concatenate([part, kvp[:, :HD], kvd[:, :HD], kvp[:, HD:], kvd[:, HD:]], axis=0)
        if d % 2:
            odd_ref[d // 2] = pack_sums(z, total, square_rows)
        else:
            even_ref[d // 2] = jnp.concatenate([total, square_rows, pad], axis=0)


def pair_sum_kernel(z, even_ref, got_ref, own_ref, *send_refs):
    for i in range(z.n // 2):
        total, squares = unpack_sums(z, got_ref[i])
        total = total + even_ref[i, 0 : z.body, :]
        squares = squares + even_ref[i, z.body : z.body + z.square_lines, :]
        if i == 0:
            pad = jnp.zeros((STAT_ROWS - z.square_lines, 128), F32)
            own_ref[...] = jnp.concatenate([total, squares, pad], axis=0)
        else:
            send_refs[-i][...] = pack_sums(z, total, squares)


def finish_kernel(z, features, own_ref, *refs):
    got_refs = refs[: z.n // 2 - 1]
    query_ref, key_ref, value_ref = refs[z.n // 2 - 1 :]
    me = lax.axis_index("ctx")
    total = own_ref[0 : z.body, :]
    squares = own_ref[z.body : z.body + z.square_lines, :]
    for ref in got_refs:
        got, got_squares = unpack_sums(z, ref[...])
        total = total + got
        squares = squares + got_squares
    inverse = lax.rsqrt(squares / features + EPSILON)
    rows = lax.broadcasted_iota(jnp.int32, (z.piece, 1), 0) + (me // z.heads) * z.piece
    query_ref[...] = (total[0 : z.piece] * rows_to_column(inverse, rows)).astype(BF16)
    slot = lax.broadcasted_iota(jnp.int32, (z.slots, 1), 0)
    late = slot - z.prompt_slots
    index = jnp.where(
        slot < z.prompt_slots,
        me * z.prompt_own + slot,
        z.prompt
        + (late // z.rows_own) * z.row_total
        + me * z.rows_own
        + late % z.rows_own,
    )
    own = rows_to_column(inverse, index)
    key_ref[...] = (total[z.piece : z.piece + z.slots] * own).astype(BF16)
    value_ref[...] = (total[z.piece + z.slots : z.piece + 2 * z.slots] * own).astype(BF16)


def prepare_kernel(z, length_ref, visible_ref, key_hbm, value_hbm, key_ref, value_ref, live_ref, extra_ref, sems):
    loads = [
        pltpu.make_async_copy(key_hbm, key_ref, sems.at[0]),
        pltpu.make_async_copy(value_hbm, value_ref, sems.at[1]),
    ]
    for load in loads:
        load.start()
    me = lax.axis_index("ctx")
    length = length_ref[0]
    size = min(BLOCK, key_ref.shape[0])
    blocks = key_ref.shape[0] // size
    local = lax.broadcasted_iota(jnp.int32, (size, HD), 0)

    def mark(i, carry):
        rows = pl.ds(pl.multiple_of(i * size, size), size)
        live_ref[rows, :] = jnp.where(local + i * size < length, 1.0, 0.0).astype(BF16)
        return carry

    lax.fori_loop(0, blocks, mark, 0)
    row = lax.broadcasted_iota(jnp.int32, (z.rows, 1), 0)
    late = row - z.prompt
    step = late // z.row_total
    place = late - step * z.row_total
    lanes = lax.broadcasted_iota(jnp.int32, (z.rows, z.row_total), 1)
    allowed = jnp.sum(
        jnp.where(lanes == place, visible_ref[...].astype(F32), 0.0), axis=1, keepdims=True
    )
    limit = jnp.where(late < 0, row + 1, allowed.astype(jnp.int32))
    slot = lax.broadcasted_iota(jnp.int32, (z.rows, z.slots), 1)
    late_slot = slot - z.prompt_slots
    from_prompt = (slot < z.prompt_own) & (me * z.prompt_own + slot < limit)
    from_decode = (
        (late_slot >= 0)
        & (late_slot < z.decode_own)
        & (late >= 0)
        & (me * z.rows_own + late_slot % z.rows_own == place)
        & (late_slot // z.rows_own <= step)
    )
    extra_ref[...] = jnp.where(from_prompt | from_decode, 0.0, MASKED)
    for load in loads:
        load.wait()
    stand_in = jnp.broadcast_to(key_ref[0:16, :].astype(F32)[0:1, :], (size, HD))

    def clear(i, carry):
        rows = pl.ds(pl.multiple_of(i * size, size), size)
        live = local + i * size < length
        key_ref[rows, :] = jnp.where(live, key_ref[rows, :].astype(F32), stand_in).astype(BF16)
        value_ref[rows, :] = jnp.where(live, value_ref[rows, :].astype(F32), 0.0).astype(BF16)
        return carry

    lax.fori_loop(length // size, blocks, clear, 0)


def beside(values, live):
    return jnp.concatenate([values, live], axis=1)


def attention_kernel(z, pieces, stacked, offset, *refs):
    key_ref, value_ref, live_ref, extra_key_ref, extra_value_ref, extra_bias_ref = refs[:6]
    if offset is None:
        query_refs = refs[6 : 6 + len(pieces)]
        out_refs = refs[6 + len(pieces) :]
    else:
        query_refs = [refs[6].at[offset + i] for i in range(len(pieces))]
        out_refs = refs[7:]
    me = lax.axis_index("ctx")
    over = (((1,), (1,)), ((), ()))
    slots = key_ref.shape[0]

    def scores(query, rows):
        return lax.dot_general(query, key_ref[rows, :], over, preferred_element_type=F32)

    def mix(weight, rows):
        return jnp.dot(
            weight.astype(BF16), beside(value_ref[rows, :], live_ref[rows, :]),
            preferred_element_type=F32,
        )

    def extras(query, d):
        half = jnp.bitwise_xor(me, d) // z.heads
        bias = extra_bias_ref[pl.ds(pl.multiple_of(half * z.piece, 8), z.piece), :]
        score = lax.dot_general(query, extra_key_ref[...], over, preferred_element_type=F32)
        return score + bias

    def mix_extras(weight):
        ones = jnp.ones((z.slots, HD), BF16)
        return jnp.dot(
            weight.astype(BF16), beside(extra_value_ref[...], ones), preferred_element_type=F32
        )

    def write(i, level, mixed):
        stats = stack_stats([column_to_rows(level * SCALE), column_to_rows(mixed[:, HD : HD + 1])])
        message = jnp.concatenate([mixed[:, :HD], stats], axis=0).astype(BF16)
        if stacked:
            out_refs[0][i] = message
        else:
            out_refs[i][...] = message

    first = min(FIRST, slots)
    chunk = min(CHUNK, slots)
    bounds = [0, first] + [k for k in range(chunk, slots + 1, chunk) if k > first]
    worst = None
    for i, d in enumerate(pieces):
        query = query_refs[i][...]
        score = scores(query, slice(0, first))
        level = jnp.max(score, axis=1, keepdims=True)
        mixed = mix(jnp.exp2((score - level) * SCALE), slice(0, first))
        for start, end in zip(bounds[1:], bounds[2:]):
            rows = slice(start, end)
            mixed = mixed + mix(jnp.exp2((scores(query, rows) - level) * SCALE), rows)
        mixed = mixed + mix_extras(jnp.exp2((extras(query, d) - level) * SCALE))
        write(i, level, mixed)
        over_limit = jnp.where(mixed[:, HD:] < TOO_LARGE, 0.0, 1.0)
        worst = over_limit if worst is None else jnp.maximum(worst, over_limit)

    @pl.when(jnp.max(worst) > 0.0)
    def _():
        for i, d in enumerate(pieces):
            query = query_refs[i][...]
            score = extras(query, d)
            level = jnp.max(score, axis=1, keepdims=True)
            mixed = mix_extras(jnp.exp2((score - level) * SCALE))

            def step(k, carry):
                level, mixed = carry
                rows = pl.ds(pl.multiple_of(k * chunk, chunk), chunk)
                score = scores(query, rows)
                higher = jnp.maximum(level, jnp.max(score, axis=1, keepdims=True))
                return higher, mixed * jnp.exp2((level - higher) * SCALE) + mix(
                    jnp.exp2((score - higher) * SCALE), rows
                )

            level, mixed = lax.fori_loop(0, slots // chunk, step, (level, mixed))
            write(i, level, mixed)


def merge(z, messages):
    blocks = []
    for message in messages:
        wide = message.astype(F32)
        top, total = read_stats(wide[z.piece :], z.stat_lines, 2)
        blocks.append((top, total, wide[0 : z.piece]))
    highest = functools.reduce(jnp.maximum, [top for top, _, _ in blocks])
    index = lax.broadcasted_iota(jnp.int32, (z.piece, 1), 0)
    total = 0.0
    mixed = 0.0
    for top, block_total, block_mixed in blocks:
        scale = jnp.exp2(top - highest)
        total = total + block_total * scale
        mixed = mixed + block_mixed * rows_to_column(scale, index)
    return highest, total, mixed


def pair_merge_kernel(z, mine_sets, got_sets, *refs):
    count = len(mine_sets) + len(got_sets)
    places = [
        [ref.at[k] for ref, size in zip(block, sizes) for k in range(size)]
        for block, sizes in ((refs, mine_sets), (refs[len(mine_sets) :], got_sets))
    ]
    for send_ref, mine_ref, got_ref in zip(refs[count:][::-1], *places):
        highest, total, mixed = merge(z, [mine_ref[...], got_ref[...]])
        send_ref[...] = jnp.concatenate([mixed, stack_stats([highest, total])], axis=0).astype(BF16)


def final_merge_kernel(z, *refs):
    out_ref = refs[-1]
    _, total, mixed = merge(z, [ref[...] for ref in refs[:-1]])
    index = lax.broadcasted_iota(jnp.int32, (z.piece, 1), 0)
    out_ref[...] = (mixed / rows_to_column(total, index)).astype(BF16)


def pack_kernel(*refs):
    for i, ref in enumerate(refs[:-1]):
        refs[-1][i] = ref[...]


def share_order(groups):
    return list(range(2, groups)) + [1, 0]


def output_products(z, weight_ref, sum_ref, pieces):
    me = lax.axis_index("ctx")
    for (d, first), (e, second) in zip(pieces[::2], pieces[1::2]):
        owners = [jnp.bitwise_xor(me, d), jnp.bitwise_xor(me, e)]
        weight = jnp.concatenate(
            [weight_ref[pl.ds(pl.multiple_of(x % z.heads * HD, HD), HD), :] for x in owners], axis=0
        )
        product = jnp.dot(
            jnp.concatenate([first[...], second[...]], axis=1), weight, preferred_element_type=F32
        )
        where = pl.ds(pl.multiple_of(owners[0] // z.heads * z.piece, 8), z.piece)
        sum_ref[where, :] = sum_ref[where, :] + product


def output_even_kernel(z, weight_ref, *refs):
    *piece_refs, sum_ref = refs
    sum_ref[...] = jnp.zeros_like(sum_ref)
    output_products(z, weight_ref, sum_ref, list(zip(range(0, z.n, 2), piece_refs)))


def output_odd_kernel(z, weight_ref, even_ref, first_ref, rest_ref, *refs):
    *out_refs, sum_ref = refs
    sum_ref[...] = even_ref[...]
    pieces = [(1, first_ref)] + [(2 * i + 3, rest_ref.at[i]) for i in range(z.n // 2 - 1)]
    output_products(z, weight_ref, sum_ref, pieces)
    place = lax.axis_index("kv")
    columns = sum_ref.shape[1]
    prompt_share = z.prompt // z.groups
    step_share = z.row_total // z.groups
    for out_ref, e in zip(out_refs, share_order(z.groups)):
        target = jnp.bitwise_xor(place, e)
        rows = [sum_ref[pl.ds(pl.multiple_of(target * prompt_share, 8), prompt_share), :]]
        for s in range(z.steps):
            start = z.prompt + s * z.row_total + target * step_share
            rows.append(sum_ref[pl.ds(pl.multiple_of(start, 8), step_share), :])
        share = jnp.concatenate(rows, axis=0)
        out_ref[...] = jnp.concatenate(
            [share[:, : columns // 2], share[:, columns // 2 :]], axis=0
        ).astype(BF16)


def share_sum_kernel(z, *refs):
    prompt_ref, step_ref = refs[z.groups :]
    total = refs[0][...].astype(F32)
    for ref in refs[1 : z.groups]:
        total = total + ref[...].astype(F32)
    prompt_share = z.prompt // z.groups
    step_share = z.row_total // z.groups
    half = total.shape[0] // 2
    columns = total.shape[1]
    for c in range(2):
        rows = total[c * half : (c + 1) * half]
        where = slice(c * columns, (c + 1) * columns)
        prompt_ref[:, where] = rows[0:prompt_share].astype(BF16)
        for s in range(z.steps):
            start = prompt_share + s * step_share
            step_ref[s, :, where] = rows[start : start + step_share].astype(BF16)


def swap(x, axis, size, d):
    return lax.ppermute(x, axis, [(i, i ^ d) for i in range(size)])


def on_device(
    prompt_in,
    step_in,
    norm_gain,
    query_weight,
    key_weight,
    value_weight,
    out_weight,
    key_cache,
    value_cache,
    cache_lengths,
    visible,
):
    n = lax.axis_size("ctx")
    groups = lax.axis_size("kv")
    z = Sizes(prompt_in, step_in, query_weight, visible, n, groups)
    pairs = n // 2

    cache_slots = key_cache.shape[1]
    cache = shape(cache_slots, HD, BF16)

    def prepare(lengths, seen):
        return call(
            functools.partial(prepare_kernel, z),
            [cache, cache, cache, shape(z.rows, z.slots, F32)],
            (lengths, seen.reshape(1, z.row_total), key_cache[0], value_cache[0]),
            "prepare",
            1e6,
            smem=1,
            far=2,
            scratch=[pltpu.SemaphoreType.DMA((2,))],
        )

    even, odd = call(
        functools.partial(project_kernel, z),
        [shape(z.project, HD, F32, pairs), shape(z.sent, HD, BF16, pairs)],
        (
            norm_gain.reshape(z.width // 128, 128),
            prompt_in,
            step_in.reshape(z.steps * z.row_total, z.width),
            query_weight,
            key_weight,
            value_weight,
        ),
        "project",
        2 * z.rows * z.width * (z.heads + 2) * HD,
        far=6,
        scratch=[
            pltpu.VMEM((z.width // 128, 128), BF16),
            pltpu.VMEM((z.prompt, z.width), BF16),
            pltpu.VMEM((z.steps * z.row_total, z.width), BF16),
            pltpu.VMEM((2, z.width // 2, z.heads * HD), BF16),
            pltpu.VMEM((z.width, HD), BF16),
            pltpu.VMEM((z.width, HD), BF16),
            pltpu.VMEM((z.rows, z.width), BF16),
            pltpu.VMEM((z.rows, z.heads * HD), F32),
            pltpu.VMEM((z.prompt, 2 * HD), F32),
            pltpu.VMEM((z.n * z.decode_slots, 2 * HD), F32),
            pltpu.SemaphoreType.DMA((7,)),
        ],
    )
    got = swap(odd, "ctx", n, 1)
    own, *sends = call(
        functools.partial(pair_sum_kernel, z),
        [shape(z.project, HD, F32)] + [shape(z.sent, HD, BF16)] * (pairs - 1),
        (even, got),
        "pair_sum",
        1e6,
    )
    visible, *sends = lax.optimization_barrier((visible, *sends))
    gots = [swap(send, "ctx", n, n - 2 * (i + 1)) for i, send in enumerate(sends)]
    keys, values, live, extra_bias = prepare(cache_lengths, visible)
    own, keys, values, live, extra_bias = lax.optimization_barrier(
        (own, keys, values, live, extra_bias)
    )
    query, extra_key, extra_value = call(
        functools.partial(finish_kernel, z, z.width * n),
        [shape(z.piece, HD, BF16), shape(z.slots, HD, BF16), shape(z.slots, HD, BF16)],
        (own, *gots),
        "finish",
        1e6,
    )

    queries = {1: swap(query, "ctx", n, 1)}
    for i in range(1, pairs):
        queries[2 * i] = swap(query, "ctx", n, 2 * i)

    def attend(pieces, stacked, name, packed=None, offset=None):
        message = shape(z.message, HD, BF16)
        outs = [shape(z.message, HD, BF16, len(pieces))] if stacked else [message] * len(pieces)
        return call(
            functools.partial(attention_kernel, z, pieces, stacked, offset),
            outs,
            (keys, values, live, extra_key, extra_value, extra_bias)
            + (tuple(queries[d] for d in pieces) if packed is None else (packed,)),
            name,
            8 * len(pieces) * z.piece * cache_slots * HD,
            )

    (first_odd,) = attend((1,), False, "attend_core")
    first_odd, *passed = lax.optimization_barrier(
        (first_odd, *[queries[2 * i] for i in range(1, pairs)])
    )
    for i in range(1, pairs):
        queries[2 * i] = passed[i - 1]
    packed = shape(z.piece, HD, BF16, pairs - 1)
    (relay,) = call(pack_kernel, [packed], tuple(passed), "pack_queries", 1e5)
    relayed = swap(relay, "ctx", n, 1)
    odd = [tuple(range(3, n, 2)[k : k + AT_ONCE]) for k in range(0, pairs - 1, AT_ONCE)]
    even = [(2,)] + [
        tuple(range(4, n, 2)[k : k + AT_ONCE]) for k in range(0, pairs - 2, AT_ONCE)
    ]
    early = attend(even[0], True, "attend_near")
    early, relayed = lax.optimization_barrier((early, relayed))
    rest_odd = [
        attend(pieces, True, f"attend_odd{k}", relayed, k * AT_ONCE)[0]
        for k, pieces in enumerate(odd)
    ]
    got_first = swap(first_odd, "ctx", n, 1)
    got_rest = [swap(block, "ctx", n, 1) for block in rest_odd]
    rest = list(early) + [
        attend(pieces, True, f"attend_even{k}")[0] for k, pieces in enumerate(even[1:])
    ]

    message = shape(z.message, HD, BF16)
    sends = call(
        functools.partial(
            pair_merge_kernel, z, [len(x) for x in even], [len(x) for x in odd]
        ),
        [message] * (pairs - 1),
        (*rest, *got_rest),
        "pair_merge",
        1e6,
    )
    query, *sends = lax.optimization_barrier((query, *sends))
    gots = [swap(send, "ctx", n, n - 2 * (i + 1)) for i, send in enumerate(sends)]
    queries[0] = query
    (own,) = attend((0,), False, "attend_own")
    (attended,) = call(
        functools.partial(final_merge_kernel, z),
        [shape(z.piece, HD, BF16)],
        (own, got_first, *gots),
        "final_merge",
        1e6,
    )
    even = [attended] + [swap(attended, "ctx", n, 2 * i) for i in range(1, pairs)]
    first_odd = swap(attended, "ctx", n, 1)
    (relay,) = call(pack_kernel, [packed], tuple(even[1:]), "pack_heads", 1e5)
    relay, *even = lax.optimization_barrier((relay, *even))
    rest_odd = swap(relay, "ctx", n, 1)

    columns = out_weight.shape[1]
    share_rows = 2 * z.rows // groups
    share = shape(share_rows, columns // 2, BF16)
    flops = z.rows * z.heads * HD * columns
    (total,) = call(
        functools.partial(output_even_kernel, z),
        [shape(z.rows, columns, F32)],
        (out_weight, *even),
        "output_even",
        flops,
    )
    shares = call(
        functools.partial(output_odd_kernel, z),
        [share] * groups,
        (out_weight, total, first_odd, rest_odd),
        "output_odd",
        flops,
        scratch=[pltpu.VMEM((z.rows, columns), F32)],
    )
    shares = [
        swap(x, "kv", groups, e) if e else x for x, e in zip(shares, share_order(groups))
    ]
    prompt_out, step_out = call(
        functools.partial(share_sum_kernel, z),
        [
            shape(z.prompt // groups, columns, BF16),
            shape(z.row_total // groups, columns, BF16, z.steps),
        ],
        tuple(shares),
        "share_sum",
        1e6,
    )
    return (prompt_out, step_out)


def solution(mesh):
    placed = (
        P(None, "ctx"),
        P(None, None, "ctx"),
        P("ctx"),
        P("ctx", "kv"),
        P("ctx", "kv"),
        P("ctx", "kv"),
        P("kv", "ctx"),
        P("kv", "ctx", None),
        P("kv", "ctx", None),
        P("ctx"),
        P(),
    )
    return jax.shard_map(
        on_device,
        mesh=mesh,
        in_specs=placed,
        out_specs=(P("kv", "ctx"), P(None, "kv", "ctx")),
        check_vma=False,
    )
```
